32 devices in a mesh: dp: 8 (over z, x), section: 4 (over y, core).
Axes of the slice: x: 2, y: 2, z: 4, core: 2. Of those that a mesh axis runs over, the one named last changes fastest.
Arguments:
- latents: bfloat16 [16, 64, 1536], P('dp', None, 'section'), may hold values from -6 to 6
- media: bfloat16 [16, 1024, 1536], P('dp'), may hold values from -6 to 6
- frames: int32 [16], P('dp'), may hold values from 1 to 8, as said below
- cotangent: bfloat16 [16, 64, 1536], P('dp', None, 'section'), may hold values from -6 to 6
- w_query: bfloat16 [2, 1536, 1536], P(None, 'dp'), may hold values from -0.15625 to 0.15625
- w_keyval: bfloat16 [2, 1536, 3072], P(None, 'dp'), may hold values from -0.15625 to 0.15625
- w_output: bfloat16 [2, 1536, 1536], P(None, 'dp'), may hold values from -1.25 to 1.25
- w_inner: bfloat16 [2, 1536, 6144], P(None, 'dp'), may hold values from -0.15625 to 0.15625
- w_outer: bfloat16 [2, 6144, 1536], P(None, 'dp'), may hold values from -0.078125 to 0.078125
- norm_gains: bfloat16 [2, 3, 1536], P(None, None, 'dp'), may hold values from 0.25 to 1.75
- norm_biases: bfloat16 [2, 3, 1536], P(None, None, 'dp'), may hold values from -1 to 1
Outputs:
- latents_out: bfloat16 [16, 64, 1536], P('dp', None, 'section')
- media_grad: float32 [16, 1024, 1536], P('dp', None, 'section')
- latents_grad: float32 [16, 64, 1536], P('dp', None, 'section')
- grad_query: float32 [2, 1536, 1536], P(None, 'dp')
- grad_keyval: float32 [2, 1536, 3072], P(None, 'dp')
- grad_output: float32 [2, 1536, 1536], P(None, 'dp')
- grad_inner: float32 [2, 1536, 6144], P(None, 'dp')
- grad_outer: float32 [2, 6144, 1536], P(None, 'dp')
- grad_gains: float32 [2, 2, 1536], P(None, None, 'dp')
- grad_biases: float32 [2, 2, 1536], P(None, None, 'dp')
- grad_ffn_norm: float32 [2, 2, 1536], P(None, None, 'dp')
The draws below stay inside these ranges and needn't reach their ends.
Inputs may be any that keep to these rules, and one draw needn't show every extreme that they name: In each aligned block of 2 videos in order, one video has 8 frames.
All inputs are finite; a program needn't handle non-finite values.
Results may differ from the reference program's by a relative error of at most 0.019.
Values may be sent and summed in bfloat16 or wider, within the bound.
No kernel may reach another device: no remote copies, remote signals or barrier semaphores. Data moves between devices by JAX's collectives and lax.ppermute only.
A program may use at most 448 MiB of HBM per device.

```python
import jax
import jax.numpy as jnp
from jax import lax

D = 1536
H = 16
FF = 6144
LAT = 64
MAXF = 8
MB = 2
LAYERS = 2
MEDIA = 1024
VIDEOS = 16


def draw_frames(key, part):
    key = jax.random.fold_in(key, 11)
    first, second = jax.random.split(key)
    counts = jax.random.randint(first, (VIDEOS,), 1, MAXF + 1)
    pick = jax.random.randint(second, (VIDEOS // MB,), 0, MB)
    full = jnp.arange(VIDEOS) % MB == jnp.repeat(pick, MB)
    return jnp.where(full, MAXF, counts).astype(jnp.int32)


def block_levels(rng, dims, cuts, low, high):
    loudness = 1.0
    for axis_at, shards_of in cuts:
        steps = jax.random.uniform(jax.random.fold_in(jax.random.fold_in(rng, 6), axis_at), (shards_of,), jnp.float32, low / len(cuts), high / len(cuts))
        loudness = loudness * jnp.repeat(jnp.exp(steps), dims[axis_at] // shards_of).reshape((-1,) + (1,) * (len(dims) - 1 - axis_at))
    return loudness


def scatter_about(stream_key, extent, scale, reach, cuts=(), held_as=jnp.bfloat16):
    level = block_levels(stream_key, extent, cuts, -0.22, 0.18) if cuts else 1.0
    values = jax.random.normal(stream_key, extent, jnp.float32) * scale * level
    return jnp.minimum(jnp.maximum(values, -reach), reach).astype(held_as)


def setup_inputs(seed: int = 0) -> dict:
    keys = jax.random.split(jax.random.key(seed), 12)
    return {
        "latents": scatter_about(keys[0], (VIDEOS, LAT, D), 1.0, 6.0, ((0, 8), (2, 4))),
        "media": scatter_about(keys[1], (VIDEOS, MEDIA, D), 1.0, 6.0, ((0, 8),)),
        "frames": draw_frames(jax.random.fold_in(keys[11], 71), 0),
        "cotangent": scatter_about(keys[3], (VIDEOS, LAT, D), 1.0, 6.0, ((0, 8), (2, 4))),
        "w_query": scatter_about(keys[4], (LAYERS, D, D), D ** -0.5, 0.15625, ((1, 8),)),
        "w_keyval": scatter_about(keys[5], (LAYERS, D, 2 * D), D ** -0.5, 0.15625, ((1, 8),)),
        "w_output": scatter_about(keys[6], (LAYERS, D, D), (D // 64) ** -0.5, 1.25, ((1, 8),)),
        "w_inner": scatter_about(keys[7], (LAYERS, D, FF), D ** -0.5, 0.15625, ((1, 8),)),
        "w_outer": scatter_about(keys[8], (LAYERS, FF, D), FF ** -0.5, 0.078125, ((1, 8),)),
        "norm_gains": jnp.clip(1.0 + 0.15 * jax.random.normal(keys[9], (LAYERS, 3, D), jnp.float32), 0.25, 1.75).astype(jnp.bfloat16),
        "norm_biases": scatter_about(keys[10], (LAYERS, 3, D), 0.2, 1.0, ((2, 8),)),
    }


@jax.custom_vjp
def low(v):
    return lax.optimization_barrier(v.astype(jnp.bfloat16)).astype(jnp.float32)

@jax.custom_vjp
def low_back(v):
    return v

def low_keep(v):
    return (low(v), None)

def low_pass(kept, grad):
    return (grad,)

def back_keep(v):
    return (v, None)

def back_low(kept, grad):
    return (low(grad),)
low.defvjp(low_keep, low_pass)
low_back.defvjp(back_keep, back_low)
eps = 1e-05
high = lax.Precision.HIGHEST

def layer_norm(value, gain, shift):
    centred = value - lax.optimization_barrier(jnp.mean(value, axis=-1, keepdims=True))
    spread = lax.optimization_barrier(jnp.mean(centred * centred, axis=-1, keepdims=True))
    return centred * lax.rsqrt(spread + eps) * gain + shift

def matmul(left, right):
    return jnp.dot(left, right, precision=high)

def one_layer(state, pictures, keep, w_query, w_keyval, w_output, w_inner, w_outer, gains, biases):
    width = state.shape[1]
    size = width // H
    scale = size ** (-0.5)
    media_norm = low(layer_norm(pictures, gains[0], biases[0]))
    lat_norm = low(layer_norm(state, gains[1], biases[1]))
    keys_in = jnp.concatenate([media_norm, lat_norm], axis=0)
    query = low(low_back(matmul(lat_norm, w_query)))
    keyval = low(low_back(matmul(keys_in, w_keyval)))
    query_h = query.reshape(-1, H, size)
    key_h = keyval[:, :width].reshape(-1, H, size)
    value_h = keyval[:, width:].reshape(-1, H, size)
    scores = low_back(jnp.einsum('qhd,khd->hqk', query_h, key_h, precision=high) * scale)
    scores = jnp.where(keep[None, None, :], scores, -1e+30)
    expo = jnp.exp(scores - lax.optimization_barrier(jnp.max(scores, axis=-1, keepdims=True)))
    probs = low(expo / lax.optimization_barrier(jnp.sum(expo, axis=-1, keepdims=True)))
    attended = jnp.einsum('hqk,khd->qhd', probs, value_h, precision=high).reshape(-1, width)
    attended = low(low_back(attended))
    mid = low_back(low(state + matmul(attended, w_output)))
    mid_norm = low(layer_norm(mid, gains[2], biases[2]))
    hidden = low_back(matmul(mid_norm, w_inner))
    active = low(jax.nn.gelu(hidden, approximate=False))
    return low(mid + low_back(matmul(active, w_outer)))

def reference(latents, media, frames, cotangent, w_query, w_keyval, w_output, w_inner, w_outer, norm_gains, norm_biases):
    params = tuple((w.astype(jnp.float32) for w in (w_query, w_keyval, w_output, w_inner, w_outer, norm_gains, norm_biases)))
    lat_len = latents.shape[1]
    media_len = media.shape[1]
    patch = media_len // MAXF

    def forward(weights, start, pictures, keep):
        state = start
        for level in range(LAYERS):
            if level > 0:
                state = low_back(state)
            state = one_layer(state, pictures, keep, *(w[level] for w in weights))
        return state

    def video(sums, item):
        start, pictures, count, target = item
        keep = jnp.concatenate([jnp.arange(media_len).astype(jnp.int32) < count * patch, jnp.ones((lat_len,), dtype=bool)])
        result, pull = jax.vjp(lambda w, s, p: forward(w, s, p, keep), params, start.astype(jnp.float32), pictures.astype(jnp.float32))
        d_weights, d_start, d_pictures = pull(target.astype(jnp.float32))
        sums = tuple((a + b for a, b in zip(sums, d_weights)))
        return (sums, (result.astype(jnp.bfloat16), d_pictures, d_start))
    init = tuple((jnp.zeros_like(w) for w in params))
    sums, stacked = lax.scan(video, init, (latents, media, frames, cotangent))
    ffn_norm = jnp.stack([sums[5][:, 2], sums[6][:, 2]], axis=1)
    return (stacked[0], stacked[1], stacked[2], sums[0], sums[1], sums[2], sums[3], sums[4], sums[5][:, :2], sums[6][:, :2], ffn_norm)
```

```python
import itertools

import jax
import jax.numpy as jnp
from jax import lax
from jax.experimental import pallas as pl
from jax.experimental.pallas import tpu as pltpu
from jax.sharding import PartitionSpec as P

H = 16
MAXF = 8
eps = 1e-05
bf16 = jnp.bfloat16
f32 = jnp.float32
AXES = ("dp", "section")


def dot(left, right):
    return jnp.dot(left, right, preferred_element_type=f32)


def dot_rows(left, right):
    return lax.dot_general(left, right, (((0,), (0,)), ((), ())), preferred_element_type=f32)


def dot_cols(left, right):
    return lax.dot_general(left, right, (((1,), (1,)), ((), ())), preferred_element_type=f32)


def at(array, index, axis=0):
    return lax.dynamic_index_in_dim(array, index, axis, keepdims=False)


def normed(value):
    centred = value - jnp.mean(value, axis=-1, keepdims=True)
    spread = jnp.mean(centred * centred, axis=-1, keepdims=True)
    rstd = lax.rsqrt(spread + eps)
    return centred * rstd, rstd


def norm_back(hat, rstd, grad):
    mean = jnp.mean(grad, axis=-1, keepdims=True)
    along = jnp.mean(grad * hat, axis=-1, keepdims=True)
    return rstd * (grad - mean - hat * along)


def place(parts, spots, count):
    total = sum(part.shape[0] for part in parts)

    def kernel(spots_ref, *refs):
        sources, out, sems = refs[:-2], refs[-2], refs[-1]
        copies = []
        for source in sources:
            for i in range(source.shape[0]):
                j = len(copies)
                copy = pltpu.make_async_copy(source.at[i], out.at[spots_ref[j]], sems.at[j])
                copy.start()
                copies.append(copy)
        for copy in copies:
            copy.wait()

    shape = parts[0].shape[1:]
    return pl.pallas_call(
        kernel,
        out_shape=jax.ShapeDtypeStruct((count,) + shape, parts[0].dtype),
        in_specs=[pl.BlockSpec(memory_space=pltpu.SMEM)]
        + [pl.BlockSpec(memory_space=pl.ANY)] * len(parts),
        out_specs=pl.BlockSpec(memory_space=pl.ANY),
        scratch_shapes=[pltpu.SemaphoreType.DMA((total,))],
    )(spots.astype(jnp.int32), *parts)


class Wires:
    def __init__(self, dp, section):
        assert section == 4 and dp % 2 == 0
        self.dp, self.section = dp, section
        self.depth = dp // 2
        self.hops = self.depth <= 4
        spots = list(itertools.product(range(self.depth), range(2), range(2), range(2)))

        def number(z, x, y, c):
            return (z * 2 + x) * section + y * 2 + c

        def pairs(move):
            return [(number(*spot), number(*move(*spot))) for spot in spots]

        n = self.depth
        self.swap_x = pairs(lambda z, x, y, c: (z, 1 - x, y, c))
        self.swap_y = pairs(lambda z, x, y, c: (z, x, 1 - y, c))
        self.swap_c = pairs(lambda z, x, y, c: (z, x, y, 1 - c))
        self.away_z = [pairs(lambda z, x, y, c, k=k: ((z + k) % n, x, y, c)) for k in range(n)]
        self.away = {
            (k, f): pairs(lambda z, x, y, c, k=k, f=f: ((z + k) % n, (x + f) % 2, y, c))
            for k in range(n)
            for f in range(2)
        }

    def enter(self):
        self.d = lax.axis_index("dp")
        self.s = lax.axis_index("section")
        self.z, self.x = self.d // 2, self.d % 2
        self.y, self.c = self.s // 2, self.s % 2

    def send(self, value, pairs):
        return lax.ppermute(value, AXES, pairs)

    def near_y(self, value):
        return self.send(value, self.swap_y)

    def near_c(self, value):
        return self.send(value, self.swap_c)

    def by_y(self, mine, other, axis):
        return jnp.where(
            self.y == 0,
            jnp.concatenate([mine, other], axis),
            jnp.concatenate([other, mine], axis),
        )

    def by_c(self, mine, other, axis):
        return jnp.where(
            self.c == 0,
            jnp.concatenate([mine, other], axis),
            jnp.concatenate([other, mine], axis),
        )

    def ring(self, k):
        return (self.z + k) % self.depth

    def gather_blocks(self, block):
        if not self.hops:
            return lax.all_gather(block, "dp", axis=0)
        n = self.depth
        got = [block] + [self.send(block, self.away_z[n - k]) for k in range(1, n)]
        here = jnp.stack(got)
        there = self.send(here, self.swap_x)
        spots = [self.ring(k) * 2 + self.x for k in range(n)]
        spots += [self.ring(k) * 2 + 1 - self.x for k in range(n)]
        return place([g[None] for g in got] + [there], jnp.stack(spots), self.dp)

    def sum_blocks(self, blocks):
        if not self.hops:
            return lax.psum_scatter(
                blocks.astype(f32), "dp", scatter_dimension=0, tiled=False
            )
        n = self.depth
        pairs = blocks.reshape((n, 2) + blocks.shape[1:])
        got = self.send(at(pairs, 1 - self.x, 1), self.swap_x)
        half = at(pairs, self.x, 1).astype(f32) + got.astype(f32)
        low = half.astype(bf16)
        total = at(half, self.z)
        for k in range(1, n):
            total = total + self.send(at(low, self.ring(k)), self.away_z[k]).astype(f32)
        return total

    def gather_rows(self, rows):
        if not self.hops:
            return lax.all_gather(rows, "dp", axis=0, tiled=True)
        n = self.depth
        got = [rows] + [self.send(rows, self.away_z[n - k]) for k in range(1, n)]
        got += [self.send(item, self.swap_x) for item in got]
        return jnp.concatenate(got, 0)

    def sum_rows(self, partial):
        if not self.hops:
            return lax.psum_scatter(partial, "dp", scatter_dimension=0, tiled=True)
        n = self.depth
        half = partial.shape[0] // 2
        got = self.send(partial[half:].astype(bf16), self.swap_x)
        near = partial[:half] + got.astype(f32)
        low = near.astype(bf16).reshape((n, half // n) + partial.shape[1:])
        total = near[: half // n]
        for k in range(1, n):
            total = total + self.send(low[k], self.away_z[k]).astype(f32)
        return total

    def trade(self, blocks):
        if not self.hops:
            mine = jnp.stack([blocks(d) for d in range(self.dp)])
            got = lax.all_to_all(mine, "dp", 0, 0, tiled=True)
            return got, jnp.arange(self.dp)
        n = self.depth
        got, order = [], []
        for f in range(2):
            for k in range(n):
                block = blocks(self.ring(k) * 2 + (self.x + f) % 2)
                got.append(block if k == f == 0 else self.send(block, self.away[k, f]))
                order.append(self.ring(n - k) * 2 + (self.x + f) % 2)
        return jnp.stack(got), jnp.stack(order)

    def spread(self, rows, fill):
        width = rows.shape[1]
        wide = at(rows.reshape(rows.shape[0], 2, width // 2), 1 - self.y, 1)
        got = self.near_y(wide.astype(bf16)).astype(fill)
        mine = at(rows.reshape(rows.shape[0], 2, width // 2), self.y, 1).astype(fill)
        return self.spread_c(self.by_y(mine, got, 0))

    def spread_c(self, cols):
        parts = cols.reshape(cols.shape[0], 2, cols.shape[1] // 2)
        got = self.near_c(at(parts, 1 - self.c, 1).astype(bf16)).astype(cols.dtype)
        return self.by_c(at(parts, self.c, 1)[None], got[None], 0)


def expand(value, heads):
    rows, width = value.shape
    size = width // heads
    owner = lax.broadcasted_iota(jnp.int32, (heads, 1, width), 2) // size
    index = lax.broadcasted_iota(jnp.int32, (heads, 1, width), 0)
    return jnp.where(owner == index, value[None], jnp.zeros((), value.dtype)).reshape(
        heads * rows, width
    )


def collapse(value, heads):
    width = value.shape[1]
    size = width // heads
    owner = lax.broadcasted_iota(jnp.int32, (heads, 1, width), 2) // size
    index = lax.broadcasted_iota(jnp.int32, (heads, 1, width), 0)
    return jnp.sum(
        jnp.where(owner == index, value.reshape(heads, -1, width), 0.0), axis=0
    )


def gelu(hidden):
    return jax.nn.gelu(hidden, approximate=False)


def shards(wires):
    def run(
        latents,
        media,
        frames,
        cotangent,
        w_query,
        w_keyval,
        w_output,
        w_inner,
        w_outer,
        norm_gains,
        norm_biases,
    ):
        wires.enter()
        y, c, s = wires.y, wires.c, wires.s
        dp = wires.dp
        layers, shard, width = w_query.shape
        size = width // H
        scale = size ** (-0.5)
        half = width // 2
        media_len = media.shape[1]
        lat_len = latents.shape[1]
        rows = lat_len // 2
        local = H // 4
        quarter = local * size

        vectors = jnp.concatenate([norm_gains, norm_biases], 1).reshape(layers * 6, shard)
        vectors = lax.all_gather(vectors, "dp", axis=1, tiled=True).astype(f32)
        vectors = vectors.reshape(layers, 2, 3, width)
        gains, biases = vectors[:, 0], vectors[:, 1]

        column = lax.broadcasted_iota(jnp.int32, (width, quarter), 1)
        row = lax.broadcasted_iota(jnp.int32, (width, quarter), 0)
        wanted = (2 * (local * c + column // size) + y) * size + column % size
        pick = (row == wanted).astype(bf16)
        stacked = jnp.stack([w_query, w_keyval[:, :, :width], w_keyval[:, :, width:]], 1)
        picked = dot(stacked.reshape(-1, width), pick).astype(bf16)
        picked = picked.reshape(layers, 3, shard, quarter)
        if wires.hops:
            out_piece = lax.dynamic_slice(
                w_output, (0, size * y, half * c), (layers, size, half)
            )

        def fetch(level):
            got = []
            if level == 0:
                for j in range(3):
                    got.append(wires.gather_blocks(picked[level, j]))
            else:
                both = jnp.concatenate([picked[level, j] for j in range(3)], 1)
                both = wires.gather_blocks(both)
                got = [both[:, :, j * quarter : (j + 1) * quarter] for j in range(3)]
            if wires.hops:
                out = wires.gather_blocks(out_piece[level]).reshape(half, half)
            else:
                out = lax.all_gather(w_output[level], "dp", axis=0, tiled=True)
                out = at(out.reshape(H // 2, 2, size, 2, half), y, 1)
                out = at(out, c, 2).reshape(half, half)
            got = [item.reshape(width, quarter) for item in got] + [out]
            far = [wires.near_c(item) for item in got]
            return [(a, b) for a, b in zip(got, far)]

        def inner_block(d):
            span = w_inner.shape[2] // dp
            part = shard // 4
            if not wires.hops:
                return w_inner[:, :, d * span : (d + 1) * span]
            return lax.dynamic_slice(w_inner, (0, part * s, span * d), (layers, part, span))

        def fetch_inner():
            got, order = wires.trade(inner_block)
            span = w_inner.shape[2] // dp
            if not wires.hops:
                return jnp.transpose(got, (1, 0, 2, 3)).reshape(layers, width, span)
            part = shard // 4
            over_y = wires.near_y(got)
            over_c, over_yc = wires.near_c(got), wires.near_c(over_y)
            spots = []
            for section in (s, s ^ 2, s ^ 1, s ^ 3):
                for i in range(dp):
                    for level in range(layers):
                        spots.append((level * dp + order[i]) * 4 + section)
            parts = [v.reshape(dp * layers, part, span) for v in (got, over_y, over_c, over_yc)]
            out = place(parts, jnp.stack(spots), layers * dp * 4)
            return out.reshape(layers, width, span)

        both = jnp.stack([latents, cotangent])
        got = wires.near_c(at(both, 1 - c, 1))
        wide = wires.by_c(at(both, c, 1), got, 2)
        whole = wires.by_y(wide, wires.near_y(wide), 2)
        whole = jnp.where(y == 0, whole, jnp.roll(whole, rows, axis=1))
        state = whole[0].astype(f32)
        target = whole[1, :rows]

        hat_f, rstd_media = normed(at(media, c).astype(f32))
        hat = hat_f.astype(bf16)
        keep = jnp.arange(media_len) < at(frames, c) * (media_len // MAXF)

        def attention(state, lat_norm, weights, level):
            (q_a, q_b), (k_a, k_b), (v_a, v_b), (o_a, o_b) = weights
            gain, bias = gains[level, 0], biases[level, 0]
            query = [dot(lat_norm, w).astype(bf16) for w in (q_a, q_b)]
            query_x = [expand(q, local) for q in query]
            lifted = jnp.concatenate([dot_cols(q, k) for q, k in zip(query_x, (k_a, k_b))], 0)
            lifted = lifted * scale
            key_g = (lifted * gain).astype(bf16)
            key_l = lifted.astype(bf16)
            shift = jnp.sum(lifted * bias, axis=-1, keepdims=True)
            scores = dot_cols(key_g, hat) + shift
            scores = jnp.where(keep[None], scores, -1e30)
            scores_l = dot_cols(key_l, lat_norm)
            top = jnp.maximum(
                jnp.max(scores, axis=-1, keepdims=True), jnp.max(scores_l, axis=-1, keepdims=True)
            )
            expo, expo_l = jnp.exp(scores - top), jnp.exp(scores_l - top)
            total = jnp.sum(expo, axis=-1, keepdims=True) + jnp.sum(expo_l, axis=-1, keepdims=True)
            probs, probs_l = expo / total, expo_l / total
            low, low_l = probs.astype(bf16), probs_l.astype(bf16)
            mass = jnp.sum(low.astype(f32), axis=-1, keepdims=True)
            mixed_hat = dot(low, hat)
            mixed = (mixed_hat * gain + mass * bias + dot(low_l, lat_norm)).astype(bf16)
            group = local * lat_len
            att = [
                collapse(dot(mixed[i * group : (i + 1) * group], v), local).astype(bf16)
                for i, v in enumerate((v_a, v_b))
            ]
            attended = wires.by_c(att[0], att[1], 1)
            branch = wires.by_c(dot(attended, o_a), dot(attended, o_b), 1)
            kept = (query, query_x, lifted, key_g, key_l, probs, probs_l, low, low_l, mass)
            return branch, kept + (mixed_hat, mixed, attended)

        def attention_back(d_mid, lat_norm, weights, level, kept):
            (q_a, q_b), (k_a, k_b), (v_a, v_b), (o_a, o_b) = weights
            query, query_x, lifted, key_g, key_l, probs, probs_l, low, low_l, mass = kept[:10]
            mixed_hat, mixed, attended = kept[10:]
            gain, bias = gains[level, 0], biases[level, 0]
            group = local * lat_len
            d_cols = d_mid.reshape(lat_len, 2, half)
            d_mine, d_other = at(d_cols, c, 1), at(d_cols, 1 - c, 1)
            d_att = (dot_cols(d_mine, o_a) + dot_cols(d_other, o_b)).astype(bf16)
            d_parts = d_att.reshape(lat_len, 2, quarter)
            d_att = [at(d_parts, c, 1), at(d_parts, 1 - c, 1)]
            d_att_x = [expand(v, local) for v in d_att]
            raised = jnp.concatenate([dot_cols(a, v) for a, v in zip(d_att_x, (v_a, v_b))], 0)
            val_g = (raised * gain).astype(bf16)
            val_l = raised.astype(bf16)
            d_probs = dot_cols(val_g, hat) + jnp.sum(raised * bias, axis=-1, keepdims=True)
            d_probs_l = dot_cols(val_l, lat_norm)
            along = jnp.sum(probs * d_probs, axis=-1, keepdims=True)
            along = along + jnp.sum(probs_l * d_probs_l, axis=-1, keepdims=True)
            ds = (probs * (d_probs - along)).astype(bf16)
            ds_l = (probs_l * (d_probs_l - along)).astype(bf16)
            ds_mass = jnp.sum(ds.astype(f32), axis=-1, keepdims=True)
            ds_hat = dot(ds, hat)
            d_lift = (ds_hat * gain + ds_mass * bias + dot(ds_l, lat_norm)).astype(bf16)
            d_query = [
                (collapse(dot(d_lift[i * group : (i + 1) * group], k), local) * scale).astype(bf16)
                for i, k in enumerate((k_a, k_b))
            ]
            d_lat = dot_cols(d_query[0], q_a) + dot_cols(d_query[1], q_b)
            d_lat = d_lat + dot_rows(
                jnp.concatenate([ds_l, low_l], 0), jnp.concatenate([key_l, val_l], 0)
            )
            d_gain = jnp.sum(lifted * ds_hat + raised * mixed_hat, axis=0)
            d_bias = jnp.sum(lifted * ds_mass + raised * mass, axis=0)
            pairs = (jnp.concatenate([ds, low], 0), jnp.concatenate([key_g, val_g], 0))
            return d_lat, (d_att, d_att_x, d_lift, d_query), (d_gain, d_bias), pairs

        def attention_grads(d_mid, lat_norm, kept, more, extra):
            query, query_x, mixed, attended = kept[0], kept[1], kept[11], kept[12]
            d_att, d_att_x, d_lift, d_query = more
            group = local * lat_len
            cols = d_mid.reshape(lat_len, 2, half)

            def both(mine, other):
                return jnp.concatenate([mine, wires.near_c(other)], 0)

            lat = both(lat_norm, lat_norm)
            mixed_b = both(mixed[:group], mixed[group:])
            d_att_b = both(d_att_x[0], d_att_x[1])
            att_b = both(attended, attended)
            d_mid_b = both(at(cols, c, 1), at(cols, 1 - c, 1))
            lift_b = both(d_lift[:group], d_lift[group:])
            query_b = both(query_x[0], query_x[1])
            d_query_b = both(d_query[0], d_query[1])
            g_value = dot_rows(mixed_b, d_att_b).astype(bf16)
            g_output = dot_rows(att_b, d_mid_b).astype(bf16)
            g_key = (dot_rows(lift_b, query_b) * scale).astype(bf16)
            g_query = dot_rows(lat, d_query_b).astype(bf16)
            parts = []
            g_query = jnp.concatenate([g_query, extra.astype(bf16)], 1)
            for grad in (g_value, g_key, g_query):
                blocks = grad.reshape(dp, shard, grad.shape[1])
                parts.append(wires.sum_blocks(blocks).astype(bf16))
            if wires.hops:
                out = wires.sum_blocks(g_output.reshape(dp, size, half)).astype(bf16)
            else:
                whole = g_output.reshape(H // 2, 1, size, half)
                zero = jnp.zeros_like(whole)
                whole = wires.by_y(whole, zero, 1)
                whole = whole.reshape(dp, shard, half)
                out = wires.sum_blocks(whole).astype(bf16)

            def join(v):
                pair = wires.by_c(v[None], wires.near_c(v)[None], 0)
                return wires.by_y(pair[None], wires.near_y(pair)[None], 0)

            value, key, query_g, out = [join(v) for v in parts + [out]]
            extra_sum = jnp.sum(query_g[..., quarter:].astype(f32), axis=(0, 1))
            query_g = query_g[..., :quarter]
            index = lax.broadcasted_iota(jnp.int32, (half, half), 0)
            goal = lax.broadcasted_iota(jnp.int32, (half, half), 1)
            head, within = index // size, index % size
            order = ((head % local) * 2 + head // local) * size + within
            shuffle = (order == goal).astype(bf16)

            def columns(v):
                v = jnp.transpose(v, (1, 2, 0, 3)).reshape(2 * shard, half)
                v = dot(v, shuffle).reshape(2, shard, half)
                return jnp.concatenate([v[0], v[1]], 1)

            g_keyval = jnp.concatenate([columns(key), columns(value)], 1)
            if wires.hops:
                g_out = jnp.transpose(out, (0, 2, 1, 3)).reshape(shard, width).astype(f32)
            else:
                g_out = jnp.sum(out.astype(f32), 0)
                g_out = jnp.concatenate([g_out[0], g_out[1]], 1)
            return columns(query_g), g_keyval, g_out, extra_sum

        def ffn_grads(active, dz_all, mn_all, d_hidden):
            span = active.shape[1]
            g_outer = dot_rows(active, dz_all).astype(bf16)
            g_inner = dot_rows(mn_all, d_hidden).astype(bf16)
            g_outer = g_outer.reshape(2, 2, span // 4, width)
            g_inner = g_inner.reshape(dp, 2, 2, shard // 4, span)

            def share(v, axis_y, axis_c):
                got = wires.near_c(at(v, 1 - c, axis_c))
                v = (at(v, c, axis_c).astype(f32) + got.astype(f32)).astype(bf16)
                got = wires.near_y(at(v, 1 - y, axis_y))
                return (at(v, y, axis_y).astype(f32) + got.astype(f32)).astype(bf16)

            g_outer = share(g_outer, 0, 1)
            g_inner = share(g_inner, 1, 2)

            def join(v):
                pair = wires.by_y(v[None], wires.near_y(v)[None], 0)
                return wires.by_c(pair[:, None], wires.near_c(pair)[:, None], 1)

            g_outer = join(g_outer).reshape(span, width).astype(f32)
            got, order = wires.trade(lambda d: at(g_inner, d))
            if wires.hops:
                got = place([got], order, dp)
            g_inner = jnp.transpose(got, (1, 0, 2)).reshape(shard // 4, dp * span)
            g_inner = join(g_inner).reshape(shard, dp * span).astype(f32)
            return g_inner, g_outer

        w_attn = [fetch(level) for level in range(layers)]
        w_in = fetch_inner()
        target_all = wires.gather_rows(target)
        x_rows = state[:rows]
        kept, norms = [], []
        for level in range(layers):
            if level == 0:
                x_hat, x_rstd = normed(state)
                lat_norm = (x_hat * gains[0, 1] + biases[0, 1]).astype(bf16)
                x_hat, x_rstd = x_hat[:rows], x_rstd[:rows]
            else:
                x_hat, x_rstd = normed(x_rows)
                mine = (x_hat * gains[level, 1] + biases[level, 1]).astype(bf16)
                lat_norm = jnp.concatenate([mine, wires.near_y(mine)], 0)
            branch, attn_kept = attention(state, lat_norm, w_attn[level], level)
            branch = branch[:rows] + wires.near_y(branch[rows:].astype(bf16)).astype(f32)
            mid = (x_rows + branch).astype(bf16).astype(f32)
            mid_hat, mid_rstd = normed(mid)
            mn = (mid_hat * gains[level, 2] + biases[level, 2]).astype(bf16)
            mn_all = wires.gather_rows(mn)
            hidden = dot(mn_all, w_in[level])
            active = gelu(hidden).astype(bf16)
            result = wires.sum_rows(dot(active, w_outer[level]))
            x_low = (mid + result).astype(bf16)
            x_rows = x_low.astype(f32)
            kept.append((attn_kept, lat_norm, x_hat, x_rstd, mid_hat, mid_rstd))
            norms.append((mn_all, hidden, active))
        latents_out = wires.spread(x_low, bf16)

        grad = target.astype(f32)
        dz_all = target_all
        zero = jnp.zeros((width,), f32)
        out_grads = [None] * layers
        media_pairs = []
        vector_grads = [None] * layers
        pending = None
        for level in reversed(range(layers)):
            attn_kept, lat_norm, x_hat, x_rstd, mid_hat, mid_rstd = kept[level]
            mn_all, hidden, active = norms[level]
            if level < layers - 1:
                dz_all = wires.gather_rows(grad.astype(bf16))
            d_active = dot_cols(dz_all, w_outer[level])
            d_hidden = jax.vjp(gelu, hidden)[1](d_active)[0].astype(bf16)
            d_mn = wires.sum_rows(dot_cols(d_hidden, w_in[level]))
            g_inner, g_outer = ffn_grads(active, dz_all, mn_all, d_hidden)
            d_mid_rows = grad + norm_back(mid_hat, mid_rstd, d_mn * gains[level, 2])
            d_low = d_mid_rows.astype(bf16)
            d_mid = jnp.concatenate([d_low, wires.near_y(d_low)], 0)
            d_lat, more, (d_gain0, d_bias0), pairs = attention_back(
                d_mid, lat_norm, w_attn[level], level, attn_kept
            )
            media_pairs.append(pairs)
            d_norm = d_lat[:rows] + wires.near_y(d_lat[rows:].astype(bf16)).astype(f32)
            grad = d_low.astype(f32) + norm_back(x_hat, x_rstd, d_norm * gains[level, 1])
            if level > 0:
                grad = grad.astype(bf16).astype(f32)
            vector_grads[level] = jnp.stack(
                [
                    d_gain0,
                    jnp.sum(d_norm * x_hat, 0),
                    jnp.sum(d_mn * mid_hat, 0),
                    d_bias0,
                    jnp.sum(d_norm, 0),
                    jnp.sum(d_mn, 0),
                ]
            )
            extra = jnp.zeros((128, width), f32).at[:6].set(vector_grads[level]).T
            g_query, g_keyval, g_out, sums = attention_grads(
                d_mid, lat_norm, attn_kept, more, extra
            )
            out_grads[level] = (g_query, g_keyval, g_out, g_inner, g_outer, sums[:, :6].T)
        latents_grad = wires.spread(grad, f32)

        left = jnp.concatenate([p[0] for p in media_pairs], 0)
        right = jnp.concatenate([p[1] for p in media_pairs], 0)
        d_media = norm_back(hat.astype(f32), rstd_media, dot_rows(left, right))
        d_media = d_media.reshape(media_len, 2, half)
        got = wires.near_y(at(d_media, 1 - y, 1).astype(bf16))
        media_grad = wires.spread_c(at(d_media, y, 1) + got.astype(f32))

        outs = [jnp.stack([out_grads[level][i] for level in range(layers)]) for i in range(6)]
        vec = outs[5].reshape(layers, 2, 3, shard)
        return (
            latents_out,
            media_grad,
            latents_grad,
            outs[0],
            outs[1],
            outs[2],
            outs[3],
            outs[4],
            vec[:, 0, :2],
            vec[:, 1, :2],
            vec[:, :, 2],
        )

    return run


def solution(mesh):
    wires = Wires(mesh.shape["dp"], mesh.shape["section"])
    return jax.shard_map(
        shards(wires),
        mesh=mesh,
        in_specs=(
            P("dp", None, "section"),
            P("dp", None, None),
            P("dp"),
            P("dp", None, "section"),
            P(None, "dp", None),
            P(None, "dp", None),
            P(None, "dp", None),
            P(None, "dp", None),
            P(None, "dp", None),
            P(None, None, "dp"),
            P(None, None, "dp"),
        ),
        out_specs=(
            P("dp", None, "section"),
            P("dp", None, "section"),
            P("dp", None, "section"),
            P(None, "dp", None),
            P(None, "dp", None),
            P(None, "dp", None),
            P(None, "dp", None),
            P(None, "dp", None),
            P(None, None, "dp"),
            P(None, None, "dp"),
            P(None, None, "dp"),
        ),
        check_vma=False,
    )
```

```python
import itertools

import jax
import jax.numpy as jnp
from jax import lax
from jax.experimental import pallas as pl
from jax.experimental.pallas import tpu as pltpu
from jax.sharding import PartitionSpec as P

H = 16
MAXF = 8
eps = 1e-05
bf16 = jnp.bfloat16
f32 = jnp.float32
AXES = ("dp", "section")


def dot(left, right):
    return jnp.dot(left, right, preferred_element_type=f32)


def dot_rows(left, right):
    return lax.dot_general(left, right, (((0,), (0,)), ((), ())), preferred_element_type=f32)


def dot_cols(left, right):
    return lax.dot_general(left, right, (((1,), (1,)), ((), ())), preferred_element_type=f32)


def at(array, index, axis=0):
    return lax.dynamic_index_in_dim(array, index, axis, keepdims=False)


def normed(value):
    centred = value - jnp.mean(value, axis=-1, keepdims=True)
    spread = jnp.mean(centred * centred, axis=-1, keepdims=True)
    rstd = lax.rsqrt(spread + eps)
    return centred * rstd, rstd


def norm_back(hat, rstd, grad):
    mean = jnp.mean(grad, axis=-1, keepdims=True)
    along = jnp.mean(grad * hat, axis=-1, keepdims=True)
    return rstd * (grad - mean - hat * along)


class Zero:
    def __init__(self, value, index):
        self.value, self.index = value, index


def gate(needed, carried=()):
    needed, carried = list(needed), list(carried)
    count = len(needed) + len(carried)

    def kernel(*refs):
        refs[count][...] = jnp.zeros((1, 1), f32)
        refs[count + 1][0, 0] = jnp.int32(0)

    anywhere = pl.BlockSpec(memory_space=pl.ANY)
    out = pl.pallas_call(
        kernel,
        out_shape=[jax.ShapeDtypeStruct((1, 1), f32), jax.ShapeDtypeStruct((1, 1), jnp.int32)]
        + [jax.ShapeDtypeStruct(v.shape, v.dtype) for v in carried],
        in_specs=[anywhere] * count,
        out_specs=[
            pl.BlockSpec(memory_space=pltpu.VMEM),
            pl.BlockSpec(memory_space=pltpu.SMEM),
        ]
        + [anywhere] * len(carried),
        input_output_aliases={len(needed) + i: i + 2 for i in range(len(carried))},
    )(*needed, *carried)
    return Zero(out[0], out[1].reshape(())), list(out[2:])


def later(value, zero):
    return value + zero.value.astype(value.dtype).reshape((1,) * value.ndim)


def line_up(blocks, order):
    rows, lanes = blocks[0].shape
    count = len(blocks)

    def kernel(order_ref, *refs):
        out = refs[-1]
        for i in range(count):
            spot = pl.multiple_of(order_ref[i] * lanes, lanes)
            out[:, pl.ds(spot, lanes)] = refs[i][...]

    return pl.pallas_call(
        kernel,
        out_shape=jax.ShapeDtypeStruct((rows, count * lanes), blocks[0].dtype),
        in_specs=[pl.BlockSpec(memory_space=pltpu.SMEM)]
        + [pl.BlockSpec(memory_space=pltpu.VMEM)] * count,
        out_specs=pl.BlockSpec(memory_space=pltpu.VMEM),
    )(jnp.stack(order).astype(jnp.int32), *blocks)


def cut(array, start, size, axis=1):
    return lax.dynamic_slice_in_dim(array, start, size, axis)


def place(blocks, spots, count):
    out = jnp.zeros((count,) + blocks[0].shape, blocks[0].dtype)
    for block, spot in zip(blocks, spots):
        out = lax.dynamic_update_index_in_dim(out, block, spot, 0)
    return out


class Wires:
    def __init__(self, dp, section):
        assert section == 4 and dp % 2 == 0
        self.dp, self.section = dp, section
        self.depth = dp // 2
        self.hops = self.depth <= 4
        spots = list(itertools.product(range(self.depth), range(2), range(2), range(2)))

        def number(z, x, y, c):
            return (z * 2 + x) * section + y * 2 + c

        def pairs(move):
            return [(number(*spot), number(*move(*spot))) for spot in spots]

        n = self.depth
        self.swap_x = pairs(lambda z, x, y, c: (z, 1 - x, y, c))
        self.swap_y = pairs(lambda z, x, y, c: (z, x, 1 - y, c))
        self.swap_c = pairs(lambda z, x, y, c: (z, x, y, 1 - c))
        self.away_z = [pairs(lambda z, x, y, c, k=k: ((z + k) % n, x, y, c)) for k in range(n)]
        self.away = {
            (k, f): pairs(lambda z, x, y, c, k=k, f=f: ((z + k) % n, (x + f) % 2, y, c))
            for k in range(n)
            for f in range(2)
        }

    def enter(self):
        self.d = lax.axis_index("dp")
        self.s = lax.axis_index("section")
        self.z, self.x = self.d // 2, self.d % 2
        self.y, self.c = self.s // 2, self.s % 2

    def send(self, value, pairs):
        return lax.ppermute(value, AXES, pairs)

    def near_y(self, value):
        return self.send(value, self.swap_y)

    def near_c(self, value):
        return self.send(value, self.swap_c)

    def by_y(self, mine, other, axis):
        return jnp.where(
            self.y == 0,
            jnp.concatenate([mine, other], axis),
            jnp.concatenate([other, mine], axis),
        )

    def by_c(self, mine, other, axis):
        return jnp.where(
            self.c == 0,
            jnp.concatenate([mine, other], axis),
            jnp.concatenate([other, mine], axis),
        )

    def ring(self, k):
        return (self.z + k) % self.depth

    def gather_near(self, block):
        n = self.depth
        return [block] + [self.send(block, self.away_z[n - k]) for k in range(1, n)]

    def gather_far(self, got):
        n = self.depth
        there = [self.send(got[0], self.swap_x)[None], self.send(jnp.stack(got[1:]), self.swap_x)]
        there = jnp.concatenate(there, 0)
        spots = [self.ring(k) * 2 + self.x for k in range(n)]
        spots += [self.ring(k) * 2 + 1 - self.x for k in range(n)]
        return place(got + [there[k] for k in range(n)], spots, self.dp)

    def sum_far(self, blocks, start=0):
        pairs = blocks.reshape((self.depth, 2) + blocks.shape[1:])
        got = self.send(at(pairs, 1 - self.x + start, 1), self.swap_x)
        return at(pairs, self.x, 1), got

    def sum_near(self, mine, got, start=0):
        half = mine.astype(f32) + got.astype(f32)
        low = half.astype(bf16)
        parts = [
            self.send(at(low, self.ring(k) + start), self.away_z[k]) for k in range(1, self.depth)
        ]
        return at(half, self.z), parts

    def gather_rows(self, rows):
        if not self.hops:
            return lax.all_gather(rows, "dp", axis=0, tiled=True)
        n = self.depth
        got = [rows] + [self.send(rows, self.away_z[n - k]) for k in range(1, n)]
        got += [self.send(item, self.swap_x) for item in got]
        return jnp.concatenate(got, 0)

    def row_order(self):
        n = self.depth
        return [self.ring(k) * 2 + (self.x + f) % 2 for f in range(2) for k in range(n)]

    def sum_rows(self, partial):
        if not self.hops:
            return lax.psum_scatter(partial, "dp", scatter_dimension=0, tiled=True)
        n = self.depth
        half = partial.shape[0] // 2
        got = self.send(partial[half:].astype(bf16), self.swap_x)
        near = partial[:half] + got.astype(f32)
        low = near.astype(bf16).reshape((n, half // n) + partial.shape[1:])
        total = near[: half // n]
        for k in range(1, n):
            total = total + self.send(low[k], self.away_z[k]).astype(f32)
        return total

    def trade_near(self, blocks):
        n = self.depth
        got = []
        for k in range(n):
            pair = [blocks(self.ring(k) * 2 + (self.x + f) % 2) for f in range(2)]
            pair = jnp.stack(pair)
            got.append(pair if k == 0 else self.send(pair, self.away_z[k]))
        return got

    def trade_far(self, got, zero):
        far = later(jnp.stack([pair[1] for pair in got]), zero)
        return [pair[0] for pair in got], self.send(far, self.swap_x)

    def trade_order(self):
        n = self.depth
        return [self.ring(n - k) * 2 + (self.x + f) % 2 for f in range(2) for k in range(n)]

    def trade_all(self, blocks):
        mine = jnp.stack([blocks(d) for d in range(self.dp)])
        return lax.all_to_all(mine, "dp", 0, 0, tiled=True)

    def spread(self, rows, fill):
        half = rows.shape[1] // 2
        got = self.near_y(cut(rows, half * (1 - self.y), half).astype(bf16)).astype(fill)
        mine = cut(rows, half * self.y, half).astype(fill)
        return self.spread_c(self.by_y(mine, got, 0))

    def spread_c(self, cols):
        half = cols.shape[1] // 2
        got = self.near_c(cut(cols, half * (1 - self.c), half).astype(bf16)).astype(cols.dtype)
        return self.by_c(cut(cols, half * self.c, half)[None], got[None], 0)


def expand(value, heads):
    rows, width = value.shape
    size = width // heads
    owner = lax.broadcasted_iota(jnp.int32, (heads, 1, width), 2) // size
    index = lax.broadcasted_iota(jnp.int32, (heads, 1, width), 0)
    return jnp.where(owner == index, value[None], jnp.zeros((), value.dtype)).reshape(
        heads * rows, width
    )


def collapse(value, heads):
    width = value.shape[1]
    size = width // heads
    owner = lax.broadcasted_iota(jnp.int32, (heads, 1, width), 2) // size
    index = lax.broadcasted_iota(jnp.int32, (heads, 1, width), 0)
    return jnp.sum(
        jnp.where(owner == index, value.reshape(heads, -1, width), 0.0), axis=0
    )


def gelu(hidden):
    return jax.nn.gelu(hidden, approximate=False)


def shards(wires):
    def run(
        latents,
        media,
        frames,
        cotangent,
        w_query,
        w_keyval,
        w_output,
        w_inner,
        w_outer,
        norm_gains,
        norm_biases,
    ):
        wires.enter()
        y, c, s = wires.y, wires.c, wires.s
        dp = wires.dp
        layers, shard, width = w_query.shape
        size = width // H
        scale = size ** (-0.5)
        half = width // 2
        media_len = media.shape[1]
        lat_len = latents.shape[1]
        rows = lat_len // 2
        local = H // 4
        quarter = local * size
        group = local * lat_len
        span = w_inner.shape[2] // dp
        part = shard // 4
        top = layers - 1

        column = lax.broadcasted_iota(jnp.int32, (width, quarter), 1)
        row = lax.broadcasted_iota(jnp.int32, (width, quarter), 0)
        wanted = (2 * (local * c + column // size) + y) * size + column % size
        pick = (row == wanted).astype(bf16)
        stacked = jnp.concatenate([w_query, w_keyval[:, :, :width], w_keyval[:, :, width:]], 1)
        picked = dot(stacked.reshape(-1, width), pick).astype(bf16)
        picked = picked.reshape(layers, 3, shard, quarter)
        vectors = jnp.concatenate([norm_gains, norm_biases], 1).reshape(layers * 6, shard)

        def inner_block(level, parts, index, start):
            count = shard // parts

            def block(d):
                at_row = count * index + start
                block = lax.dynamic_slice(w_inner, (level, at_row, span * d), (1, count, span))
                return block[0]

            return block

        def weights_of(whole):
            whole = whole.reshape(-1, whole.shape[2])
            return [whole, wires.near_c(whole)]

        def joined(whole):
            whole = whole.reshape(dp, 2, size, quarter)
            return jnp.concatenate([whole[:, h].reshape(half, quarter) for h in range(2)], 1)[None]

        w_attn = [None] * layers
        if wires.hops:
            out_piece = lax.dynamic_slice(
                w_output, (0, size * y, half * c), (layers, size, half)
            )
            padded = jnp.zeros((128, shard), bf16).at[: layers * 6].set(vectors)
            first = jnp.concatenate([picked[0, 0], picked[0, 1], padded.T], 1)
            first = wires.gather_near(first)
            out_piece = jnp.concatenate([out_piece[..., :quarter], out_piece[..., quarter:]], 1)
            second = lax.all_gather(jnp.stack([picked[0, 2], out_piece[0]]), "dp", axis=1)
            zero, _ = gate(first[1:])
            inner0 = wires.trade_near(inner_block(0, 2, c, zero.index))
            first = wires.gather_far(first)
            first = [first[:, :, i * quarter : (i + 1) * quarter] for i in range(2)] + [
                first[:, :, 2 * quarter :]
            ]
            one = lax.broadcasted_iota(jnp.int32, (layers * 6, 128), 0)
            one = (one == lax.broadcasted_iota(jnp.int32, (layers * 6, 128), 1)).astype(bf16)
            vectors = dot_cols(one, first[2].reshape(width, 128))
        else:
            vectors = lax.all_gather(vectors, "dp", axis=1, tiled=True)
        vectors = vectors.astype(f32).reshape(layers, 2, 3, width)
        gains, biases = vectors[:, 0], vectors[:, 1]

        both = jnp.stack([latents, cotangent])
        got = wires.near_c(at(both, 1 - c, 1))
        wide = wires.by_c(at(both, c, 1), got, 2)
        whole = wires.by_y(wide, wires.near_y(wide), 2)
        whole = jnp.where(y == 0, whole, jnp.roll(whole, rows, axis=1))
        state = whole[0].astype(f32)
        target = whole[1, :rows]

        hat_f, rstd_media = normed(at(media, c).astype(f32))
        hat = hat_f.astype(bf16)
        keep = jnp.arange(media_len) < at(frames, c) * (media_len // MAXF)

        def look(lat_norm, w_q, w_k, level):
            gain, bias = gains[level, 0], biases[level, 0]
            query = [dot(lat_norm, w).astype(bf16) for w in w_q]
            query_x = [expand(q, local) for q in query]
            lifted = jnp.concatenate([dot_cols(q, k) for q, k in zip(query_x, w_k)], 0)
            lifted = lifted * scale
            key_g = (lifted * gain).astype(bf16)
            key_l = lifted.astype(bf16)
            shift = jnp.sum(lifted * bias, axis=-1, keepdims=True)
            scores = dot_cols(key_g, hat) + shift
            scores = jnp.where(keep[None], scores, -1e30)
            scores_l = dot_cols(key_l, lat_norm)
            high = jnp.maximum(
                jnp.max(scores, axis=-1, keepdims=True), jnp.max(scores_l, axis=-1, keepdims=True)
            )
            expo, expo_l = jnp.exp(scores - high), jnp.exp(scores_l - high)
            total = jnp.sum(expo, axis=-1, keepdims=True) + jnp.sum(expo_l, axis=-1, keepdims=True)
            low, low_l = (expo / total).astype(bf16), (expo_l / total).astype(bf16)
            mass = jnp.sum(low.astype(f32), axis=-1, keepdims=True)
            mixed_hat = dot(low, hat)
            mixed = (mixed_hat * gain + mass * bias + dot(low_l, lat_norm)).astype(bf16)
            mixed_hat = mixed_hat.astype(bf16)
            return dict(
                query=query, query_x=query_x, key_g=key_g, key_l=key_l,
                low=low, low_l=low_l, mass=mass, mixed_hat=mixed_hat, mixed=mixed,
            )

        def answer(kept, w_v, w_o):
            mixed = kept["mixed"]
            att = [
                collapse(dot(mixed[i * group : (i + 1) * group], v), local).astype(bf16)
                for i, v in enumerate(w_v)
            ]
            attended = wires.by_c(att[0], att[1], 1)
            kept["attended"] = attended
            return wires.by_c(dot(attended, w_o[0]), dot(attended, w_o[1]), 1)

        def answer_back(d_mid, lat_norm, weights, level, kept):
            w_v, w_o = weights[2], weights[3]
            gain, bias = gains[level, 0], biases[level, 0]
            d_mine, d_other = cut(d_mid, half * c, half), cut(d_mid, half * (1 - c), half)
            d_att = (dot_cols(d_mine, w_o[0]) + dot_cols(d_other, w_o[1])).astype(bf16)
            d_att = [cut(d_att, quarter * c, quarter), cut(d_att, quarter * (1 - c), quarter)]
            d_att_x = [expand(v, local) for v in d_att]
            raised = jnp.concatenate([dot_cols(a, v) for a, v in zip(d_att_x, w_v)], 0)
            val_g = (raised * gain).astype(bf16)
            val_l = raised.astype(bf16)
            shift = jnp.sum(raised * bias, axis=-1, keepdims=True)
            kept.update(d_att=d_att, d_att_x=d_att_x, val_g=val_g, val_l=val_l)
            kept.update(shift=shift, d_mine=d_mine, d_other=d_other)

        def look_back(lat_norm, weights, level, kept):
            w_q, w_k = weights[0], weights[1]
            gain, bias = gains[level, 0], biases[level, 0]
            probs, probs_l = kept["low"].astype(f32), kept["low_l"].astype(f32)
            d_probs = dot_cols(kept["val_g"], hat) + kept["shift"]
            d_probs_l = dot_cols(kept["val_l"], lat_norm)
            along = jnp.sum(probs * d_probs, axis=-1, keepdims=True)
            along = along + jnp.sum(probs_l * d_probs_l, axis=-1, keepdims=True)
            ds = (probs * (d_probs - along)).astype(bf16)
            ds_l = (probs_l * (d_probs_l - along)).astype(bf16)
            ds_mass = jnp.sum(ds.astype(f32), axis=-1, keepdims=True)
            ds_hat = dot(ds, hat)
            d_lift = (ds_hat * gain + ds_mass * bias + dot(ds_l, lat_norm)).astype(bf16)
            d_query = [
                (collapse(dot(d_lift[i * group : (i + 1) * group], k), local) * scale).astype(bf16)
                for i, k in enumerate(w_k)
            ]
            d_lat = dot_cols(d_query[0], w_q[0]) + dot_cols(d_query[1], w_q[1])
            d_lat = d_lat + dot_rows(
                jnp.concatenate([ds_l, kept["low_l"]], 0),
                jnp.concatenate([kept["key_l"], kept["val_l"]], 0),
            )
            lifted, raised = kept["key_l"].astype(f32), kept["val_l"].astype(f32)
            d_gain = jnp.sum(lifted * ds_hat + raised * kept["mixed_hat"].astype(f32), axis=0)
            d_bias = jnp.sum(lifted * ds_mass + raised * kept["mass"], axis=0)
            kept.update(ds=ds, d_lift=d_lift, d_query=d_query, d_gain=d_gain, d_bias=d_bias)
            return d_lat

        def value_grads(kept, zero):
            small = [kept["attended"], kept["d_other"], kept["d_att"][1]]
            got = wires.near_c(later(jnp.concatenate(small, 1), zero))
            attended, d_mine, d_att = got[:, :half], got[:, half:width], got[:, width:]
            mixed = wires.near_c(later(kept["mixed"][group:], zero))
            mixed = jnp.concatenate([kept["mixed"][:group], mixed], 0)
            d_att = jnp.concatenate([kept["d_att_x"][0], expand(d_att, local)], 0)
            g_value = dot_rows(mixed, d_att).astype(bf16)
            attended = jnp.concatenate([kept["attended"], attended], 0)
            d_mine = jnp.concatenate([kept["d_mine"], d_mine], 0)
            g_output = dot_rows(attended, d_mine).astype(bf16)
            return [g_value, g_output]

        def query_grads(lat_norm, kept, zero):
            small = [lat_norm, kept["query"][1], kept["d_query"][1]]
            got = wires.near_c(later(jnp.concatenate(small, 1), zero))
            lat, query, d_query = got[:, :width], got[:, width : width + quarter], got[:, width + quarter :]
            lift = wires.near_c(later(kept["d_lift"][group:], zero))
            lift = jnp.concatenate([kept["d_lift"][:group], lift], 0)
            query = jnp.concatenate([kept["query_x"][0], expand(query, local)], 0)
            g_key = (dot_rows(lift, query) * scale).astype(bf16)
            lat = jnp.concatenate([lat_norm, lat], 0)
            d_query = jnp.concatenate([kept["d_query"][0], d_query], 0)
            return [dot_rows(lat, d_query).astype(bf16), g_key]

        index = lax.broadcasted_iota(jnp.int32, (half, half), 0)
        goal = lax.broadcasted_iota(jnp.int32, (half, half), 1)
        head, within = index // size, index % size
        order = ((head % local) * 2 + head // local) * size + within
        shuffle = (order == goal).astype(bf16)

        def columns(v):
            n = v.shape[2]
            both = [jnp.concatenate([v[0, i], v[1, i]], 1) for i in range(2)]
            out = dot(jnp.concatenate(both, 0), shuffle)
            return jnp.concatenate([out[:n], out[n:]], 1)

        def finish(query, key, value, out):
            out = jnp.concatenate([out[:, 0], out[:, 1]], 2).reshape(shard, width).astype(f32)
            key_value = jnp.concatenate([columns(key), columns(value)], 1)
            return columns(query), key_value, out

        def finish_generic(query_key, g_value, g_output):
            blocks = jnp.concatenate(query_key + [g_value], 1).reshape(dp, shard, 3 * quarter)
            parts = lax.psum_scatter(blocks, "dp", scatter_dimension=0, tiled=False)
            whole = g_output.reshape(H // 2, 1, size, half)
            whole = wires.by_y(whole, jnp.zeros_like(whole), 1).reshape(dp, shard, half)
            out = lax.psum_scatter(whole, "dp", scatter_dimension=0, tiled=False)
            parts = lax.all_gather(parts, "section", axis=0).reshape(2, 2, shard, 3 * quarter)
            out = lax.all_gather(out, "section", axis=0).reshape(2, 2, shard, half)
            out = jnp.sum(out.astype(f32), 0)
            parts = [columns(parts[..., j * quarter : (j + 1) * quarter]) for j in range(3)]
            out = jnp.concatenate([out[0], out[1]], 1)
            return parts[0], jnp.concatenate(parts[1:], 1), out

        def ffn_grads(active, dz_all, mn_all, d_hidden):
            g_inner = dot_rows(mn_all, d_hidden).astype(bf16)
            return g_inner, dot_rows(active, dz_all).astype(bf16)

        def norm_latents(x_hat, level):
            return (x_hat * gains[level, 1] + biases[level, 1]).astype(bf16)

        def middle(x_rows, branch, level):
            branch = branch[:rows] + wires.near_y(branch[rows:].astype(bf16)).astype(f32)
            mid = (x_rows + branch).astype(bf16).astype(f32)
            hat_m, rstd_m = normed(mid)
            mn = (hat_m * gains[level, 2] + biases[level, 2]).astype(bf16)
            return mid, hat_m, rstd_m, mn

        def ffn_back(dz_all, hidden, level):
            d_active = dot_cols(dz_all, w_outer[level])
            return jax.vjp(gelu, hidden)[1](d_active)[0].astype(bf16)

        def middle_back(grad, hat_m, rstd_m, d_mn, level):
            d_low = (grad + norm_back(hat_m, rstd_m, d_mn * gains[level, 2])).astype(bf16)
            return d_low, jnp.concatenate([d_low, wires.near_y(d_low)], 0)

        def latents_back(d_low, d_lat, x_hat, x_rstd, level):
            d_norm = d_lat[:rows] + wires.near_y(d_lat[rows:].astype(bf16)).astype(f32)
            grad = d_low.astype(f32) + norm_back(x_hat, x_rstd, d_norm * gains[level, 1])
            if level > 0:
                grad = grad.astype(bf16).astype(f32)
            return d_norm, grad

        def vector_rows(attn, d_norm, x_hat, d_mn, hat_m):
            return [
                attn["d_gain"],
                jnp.sum(d_norm * x_hat, 0),
                jnp.sum(d_mn * hat_m, 0),
                attn["d_bias"],
                jnp.sum(d_norm, 0),
                jnp.sum(d_mn, 0),
            ]

        def media_pair(attn):
            left = jnp.concatenate([attn["ds"], attn["low"]], 0)
            return left, jnp.concatenate([attn["key_g"], attn["val_g"]], 0)

        def outputs(x_low, grad, media_grad, attn_out, ffn_out, sums):
            sums = sums.reshape(layers, 2, 3, shard)
            outs = [jnp.stack([attn_out[level][i] for level in range(layers)]) for i in range(3)]
            outs += [jnp.stack([ffn_out[level][i] for level in range(layers)]) for i in range(2)]
            return (
                wires.spread(x_low, bf16),
                media_grad,
                wires.spread(grad, f32),
                *outs,
                sums[:, 0, :2],
                sums[:, 1, :2],
                sums[:, :, 2],
            )

        x_hat0, x_rstd0 = normed(state)
        lat_norm0 = norm_latents(x_hat0, 0)
        x_hat0, x_rstd0 = x_hat0[:rows], x_rstd0[:rows]
        x_rows0 = state[:rows]

        if not wires.hops:
            nil = Zero(jnp.zeros((1, 1), f32), 0)
            x_rows, x_hat, x_rstd, lat_norm = x_rows0, x_hat0, x_rstd0, lat_norm0
            kept = []
            for level in range(layers):
                got = [
                    lax.all_gather(picked[level, j], "dp", axis=0).reshape(width, quarter)
                    for j in range(3)
                ]
                out = lax.all_gather(w_output[level], "dp", axis=0, tiled=True)
                out = at(out.reshape(H // 2, 2, size, 2, half), y, 1)
                got.append(at(out, c, 2).reshape(half, half))
                weights = [[item, wires.near_c(item)] for item in got]
                w_in = wires.trade_all(inner_block(level, 1, 0, 0)).reshape(width, span)
                if level > 0:
                    x_hat, x_rstd = normed(x_rows)
                    mine = norm_latents(x_hat, level)
                    lat_norm = jnp.concatenate([mine, wires.near_y(mine)], 0)
                attn = look(lat_norm, weights[0], weights[1], level)
                branch = answer(attn, weights[2], weights[3])
                mid, hat_m, rstd_m, mn = middle(x_rows, branch, level)
                mn_all = wires.gather_rows(mn)
                hidden = dot(mn_all, w_in)
                active = gelu(hidden).astype(bf16)
                x_low = (mid + wires.sum_rows(dot(active, w_outer[level]))).astype(bf16)
                x_rows = x_low.astype(f32)
                kept.append(
                    (attn, lat_norm, x_hat, x_rstd, hat_m, rstd_m, mn_all, hidden, active, weights, w_in)
                )
            grad = target.astype(f32)
            ffn_out, attn_out, vector_grads, media_sum = [], [], [], 0.0
            for level in reversed(range(layers)):
                attn, lat_norm, x_hat, x_rstd, hat_m, rstd_m, mn_all, hidden, active, weights, w_in = kept[level]
                dz_all = wires.gather_rows(grad.astype(bf16))
                d_hidden = ffn_back(dz_all, hidden, level)
                d_mn = wires.sum_rows(dot_cols(d_hidden, w_in))
                share = ffn_grads(active, dz_all, mn_all, d_hidden)
                share = [lax.psum(v.astype(f32), "section") for v in share]
                inner = share[0].reshape(dp, shard, span).astype(bf16)
                inner = wires.trade_all(lambda d: inner[d])
                inner = jnp.transpose(inner, (1, 0, 2)).reshape(shard, dp * span)
                ffn_out.insert(0, (inner.astype(f32), share[1]))
                d_low, d_mid = middle_back(grad, hat_m, rstd_m, d_mn, level)
                answer_back(d_mid, lat_norm, weights, level, attn)
                d_lat = look_back(lat_norm, weights, level, attn)
                d_norm, grad = latents_back(d_low, d_lat, x_hat, x_rstd, level)
                vector_grads = vector_rows(attn, d_norm, x_hat, d_mn, hat_m) + vector_grads
                attn_out.insert(
                    0, finish_generic(query_grads(lat_norm, attn, nil), *value_grads(attn, nil))
                )
                media_sum = media_sum + dot_rows(*media_pair(attn))
            d_media = norm_back(hat.astype(f32), rstd_media, media_sum)
            got = wires.near_y(cut(d_media, half * (1 - y), half).astype(bf16))
            media_grad = wires.spread_c(cut(d_media, half * y, half) + got.astype(f32))
            extra = lax.psum(jnp.stack(vector_grads), "section")
            sums = lax.psum_scatter(extra, "dp", scatter_dimension=1, tiled=True)
            return outputs(x_low, grad, media_grad, attn_out, ffn_out, sums)

        order = wires.trade_order()
        w_q, w_k = [weights_of(v) for v in first[:2]]
        attn0 = look(lat_norm0, w_q, w_k, 0)
        zero, (second,) = gate([attn0["low"]] + inner0[1:], [second])
        piece = jnp.concatenate([picked[1], out_piece[1][None]], 0)
        rest = lax.all_gather(later(piece, zero), "dp", axis=1)
        inner0 = wires.trade_far(inner0, zero)
        w_v, w_o = [weights_of(v) for v in (second[0], joined(second[1]))]
        weights0 = [w_q, w_k, w_v, w_o]
        branch = answer(attn0, w_v, w_o)
        zero, (branch,) = gate([inner0[1]], [branch])
        step = zero.index
        mid0, hat_m0, rstd_m0, mn = middle(x_rows0, branch, 0)
        mn_all0 = wires.gather_rows(mn)
        inner0 = place(inner0[0] + list(inner0[1]), [v + step for v in order], dp)
        inner0 = wires.by_c(inner0[:, None], wires.near_c(inner0)[:, None], 1)
        w_in0 = inner0.reshape(width, span)
        hidden0 = dot(mn_all0, w_in0)
        active0 = gelu(hidden0).astype(bf16)
        x_low = (mid0 + wires.sum_rows(dot(active0, w_outer[0]))).astype(bf16)

        zero, (x_low, rest) = gate([], [x_low, rest])
        inner1 = wires.trade_near(inner_block(1, 4, s, zero.index))
        targets = wires.gather_near(later(target, zero))
        x_rows1 = x_low.astype(f32)
        x_hat1, x_rstd1 = normed(x_rows1)
        mine = norm_latents(x_hat1, 1)
        lat_norm1 = jnp.concatenate([mine, wires.near_y(mine)], 0)
        weights1 = [weights_of(v) for v in (rest[0], rest[1], rest[2], joined(rest[3]))]
        attn1 = look(lat_norm1, weights1[0], weights1[1], 1)
        zero, _ = gate([attn1["low"]])
        inner1 = wires.trade_far(inner1, zero)
        targets = later(jnp.concatenate(targets, 0), zero)
        target_all = jnp.concatenate([targets, wires.send(targets, wires.swap_x)], 0)
        branch = answer(attn1, weights1[2], weights1[3])
        zero, (branch,) = gate([], [branch])
        step = zero.index
        mid1, hat_m1, rstd_m1, mn = middle(x_rows1, branch, 1)
        mn_all1 = wires.gather_rows(mn)
        inner1 = place(inner1[0] + list(inner1[1]), [v + step for v in order], dp)
        inner1 = wires.by_y(inner1[:, None], wires.near_y(inner1)[:, None], 1)
        inner1 = wires.by_c(inner1[:, :, None], wires.near_c(inner1)[:, :, None], 2)
        w_in1 = inner1.reshape(width, span)
        hidden1 = dot(mn_all1, w_in1)
        active1 = gelu(hidden1).astype(bf16)
        x_part = dot(active1, w_outer[1]).astype(bf16)

        d_hidden = ffn_back(target_all, hidden1, 1)
        d_mn1 = wires.sum_rows(dot_cols(d_hidden, w_in1))
        g_ffn = ffn_grads(active1, target_all, mn_all1, d_hidden)
        zero, (d_mn1,) = gate(g_ffn, [d_mn1])

        def shared(grads):
            g_inner = jnp.transpose(grads[0].reshape(dp, 4, part, span), (1, 0, 2, 3))
            parts = [g_inner, grads[1].reshape(4, span // 4, width)]
            return [lax.psum_scatter(v, "section", scatter_dimension=0) for v in parts]

        def output_blocks(grad):
            grad = grad.reshape(dp, size, half)
            return jnp.concatenate([grad[:, :, :quarter], grad[:, :, quarter:]], 1)

        def output_columns(v):
            v = v.reshape(2, 2, 2, size, quarter)
            return jnp.concatenate([v[:, :, 0], v[:, :, 1]], 3)

        share1 = shared(g_ffn)
        d_low1, d_mid1 = middle_back(target.astype(f32), hat_m1, rstd_m1, d_mn1, 1)
        answer_back(d_mid1, lat_norm1, weights1, 1, attn1)
        d_lat = look_back(lat_norm1, weights1, 1, attn1)
        zero, (d_lat,) = gate([], [d_lat])
        d_norm1, grad = latents_back(d_low1, d_lat, x_hat1, x_rstd1, 1)
        dz_all = wires.gather_rows(grad.astype(bf16))
        g_attn = query_grads(lat_norm1, attn1, zero) + value_grads(attn1, zero)

        zero, (dz_all,) = gate(g_attn, [dz_all])
        blocks = [v.reshape(dp, shard, quarter) for v in g_attn[:3]] + [output_blocks(g_attn[3])]
        blocks = jnp.concatenate(blocks, 2)
        blocks1 = lax.psum_scatter(blocks, "dp", scatter_dimension=0, tiled=False)
        d_hidden = ffn_back(dz_all, hidden0, 0)
        d_mn0 = wires.sum_rows(dot_cols(d_hidden, w_in0))
        g_ffn = ffn_grads(active0, dz_all, mn_all0, d_hidden)
        left, right = media_pair(attn1)
        media_sum = dot_rows(left, later(right, zero))
        zero, (d_mn0, *g_ffn) = gate([media_sum, *share1], [d_mn0, *g_ffn])
        share0 = shared(g_ffn)
        d_low0, d_mid0 = middle_back(grad, hat_m0, rstd_m0, d_mn0, 0)
        answer_back(d_mid0, lat_norm0, weights0, 0, attn0)
        g_vo = value_grads(attn0, zero)
        zero, (attn0["shift"],) = gate(g_vo, [attn0["shift"]])
        g_vo = jnp.concatenate([g_vo[0].reshape(dp, shard, quarter), output_blocks(g_vo[1])], 2)
        g_vo = wires.sum_far(g_vo, zero.index)
        d_lat = look_back(lat_norm0, weights0, 0, attn0)
        zero, (d_lat, attn0["d_lift"]) = gate([], [d_lat, attn0["d_lift"]])
        g_vo = wires.sum_near(g_vo[0], later(g_vo[1], zero))
        d_norm0, grad = latents_back(d_low0, d_lat, x_hat0, x_rstd0, 0)
        left, right = media_pair(attn0)
        media_sum = media_sum + dot_rows(left, later(right, zero))
        d_media = norm_back(hat.astype(f32), rstd_media, media_sum)
        send = cut(d_media, half * (1 - y), half).astype(bf16)
        zero, (send, grad, attn0["d_lift"]) = gate([], [send, grad, attn0["d_lift"]])
        got = wires.near_y(send)
        extra = vector_rows(attn0, d_norm0, x_hat0, d_mn0, hat_m0)
        extra += vector_rows(attn1, d_norm1, x_hat1, d_mn1, hat_m1)
        extra = jnp.zeros((128, width), f32).at[: layers * 6].set(jnp.stack(extra)).T
        g_qk = query_grads(lat_norm0, attn0, zero) + [extra.astype(bf16)]
        g_qk = jnp.concatenate(g_qk, 1)
        zero, (g_qk, blocks1, *share1) = gate([], [g_qk, blocks1, *share1])
        step = zero.index
        g_qk = wires.sum_far(g_qk.reshape(dp, shard, g_qk.shape[1]), step)
        x_part = wires.sum_rows(later(x_part, zero).astype(f32))
        blocks1 = lax.all_gather(blocks1, "section", axis=0)
        outer1 = lax.all_gather(share1[1], "section", axis=0, tiled=True)
        zero, (far, grad, share0[0]) = gate([], [g_qk[1], grad, share0[0]])
        step = zero.index
        g_qk = wires.sum_near(g_qk[0], far)
        trade = jnp.concatenate([share1[0], share0[0]], 1)
        trade = wires.trade_near(lambda d: at(trade, d + step))
        blocks1 = later(blocks1, zero).reshape(2, 2, shard, 4 * quarter)
        parts = [blocks1[..., j * quarter : (j + 1) * quarter] for j in range(4)]
        attn_out1 = finish(*parts[:3], output_columns(parts[3]))
        zero, (grad, share0[1], *arrived) = gate([*attn_out1], [grad, share0[1], *g_qk[1]])
        g_qk = (g_qk[0], arrived)
        trade = wires.trade_far(trade, zero)
        outer0 = lax.all_gather(share0[1], "section", axis=0, tiled=True)
        x_out = (mid1 + x_part + zero.value).astype(bf16)

        def summed(mine, parts):
            for v in parts:
                mine = mine + v.astype(f32)
            return mine.astype(bf16)

        def join(v):
            pair = wires.by_y(v[None], wires.near_y(v)[None], 0)
            return wires.by_c(pair[:, None], wires.near_c(pair)[:, None], 1)

        four = join(jnp.concatenate([summed(*g_vo), summed(*g_qk)], 1))
        value, out, query, key = [four[..., i * quarter : (i + 1) * quarter] for i in range(4)]
        sums = jnp.sum(four[..., 4 * quarter :].astype(f32), axis=(0, 1))[:, : layers * 6].T
        inner = []
        for i in range(layers):
            rows_of = slice(i * part, (i + 1) * part)
            blocks = [v[rows_of] for v in trade[0] + list(trade[1])]
            v = lax.all_gather(line_up(blocks, order), "section", axis=0, tiled=True)
            inner.append(v.astype(f32))
        ffn_out = [(inner[1], outer0.astype(f32)), (inner[0], outer1.astype(f32))]
        attn_out0 = finish(query, key, value, output_columns(out))
        media_grad = wires.spread_c(cut(d_media, half * y, half) + later(got, zero).astype(f32))
        return outputs(
            x_out, grad, media_grad, [attn_out0, attn_out1], ffn_out, sums
        )

    return run


def solution(mesh):
    wires = Wires(mesh.shape["dp"], mesh.shape["section"])
    return jax.shard_map(
        shards(wires),
        mesh=mesh,
        in_specs=(
            P("dp", None, "section"),
            P("dp", None, None),
            P("dp"),
            P("dp", None, "section"),
            P(None, "dp", None),
            P(None, "dp", None),
            P(None, "dp", None),
            P(None, "dp", None),
            P(None, "dp", None),
            P(None, None, "dp"),
            P(None, None, "dp"),
        ),
        out_specs=(
            P("dp", None, "section"),
            P("dp", None, "section"),
            P("dp", None, "section"),
            P(None, "dp", None),
            P(None, "dp", None),
            P(None, "dp", None),
            P(None, "dp", None),
            P(None, "dp", None),
            P(None, None, "dp"),
            P(None, None, "dp"),
            P(None, None, "dp"),
        ),
        check_vma=False,
    )
```

```python
import itertools

import jax
import jax.numpy as jnp
from jax import lax
from jax.experimental import pallas as pl
from jax.experimental.pallas import tpu as pltpu
from jax.sharding import PartitionSpec as P

H = 16
MAXF = 8
eps = 1e-05
bf16 = jnp.bfloat16
f32 = jnp.float32
AXES = ("dp", "section")


def dot(left, right):
    return jnp.dot(left, right, preferred_element_type=f32)


def dot_rows(left, right):
    return lax.dot_general(left, right, (((0,), (0,)), ((), ())), preferred_element_type=f32)


def dot_cols(left, right):
    return lax.dot_general(left, right, (((1,), (1,)), ((), ())), preferred_element_type=f32)


def at(array, index, axis=0):
    return lax.dynamic_index_in_dim(array, index, axis, keepdims=False)


def normed(value):
    centred = value - jnp.mean(value, axis=-1, keepdims=True)
    spread = jnp.mean(centred * centred, axis=-1, keepdims=True)
    rstd = lax.rsqrt(spread + eps)
    return centred * rstd, rstd


def norm_back(hat, rstd, grad):
    mean = jnp.mean(grad, axis=-1, keepdims=True)
    along = jnp.mean(grad * hat, axis=-1, keepdims=True)
    return rstd * (grad - mean - hat * along)


class Zero:
    def __init__(self, value, index):
        self.value, self.index = value, index


def gate(needed, carried=()):
    needed, carried = list(needed), list(carried)
    count = len(needed) + len(carried)

    def kernel(*refs):
        refs[count][...] = jnp.zeros((1, 1), f32)
        refs[count + 1][0, 0] = jnp.int32(0)

    anywhere = pl.BlockSpec(memory_space=pl.ANY)
    out = pl.pallas_call(
        kernel,
        out_shape=[jax.ShapeDtypeStruct((1, 1), f32), jax.ShapeDtypeStruct((1, 1), jnp.int32)]
        + [jax.ShapeDtypeStruct(v.shape, v.dtype) for v in carried],
        in_specs=[anywhere] * count,
        out_specs=[
            pl.BlockSpec(memory_space=pltpu.VMEM),
            pl.BlockSpec(memory_space=pltpu.SMEM),
        ]
        + [anywhere] * len(carried),
        input_output_aliases={len(needed) + i: i + 2 for i in range(len(carried))},
    )(*needed, *carried)
    return Zero(out[0], out[1].reshape(())), list(out[2:])


def later(value, zero):
    return value + zero.value.astype(value.dtype).reshape((1,) * value.ndim)


def line_up(blocks, order):
    rows, lanes = blocks[0].shape
    count = len(blocks)

    def kernel(order_ref, *refs):
        out = refs[-1]
        for i in range(count):
            spot = pl.multiple_of(order_ref[i] * lanes, lanes)
            out[:, pl.ds(spot, lanes)] = refs[i][...]

    return pl.pallas_call(
        kernel,
        out_shape=jax.ShapeDtypeStruct((rows, count * lanes), blocks[0].dtype),
        in_specs=[pl.BlockSpec(memory_space=pltpu.SMEM)]
        + [pl.BlockSpec(memory_space=pltpu.VMEM)] * count,
        out_specs=pl.BlockSpec(memory_space=pltpu.VMEM),
    )(jnp.stack(order).astype(jnp.int32), *blocks)


def cut(array, start, size, axis=1):
    return lax.dynamic_slice_in_dim(array, start, size, axis)


def place(blocks, spots, count):
    out = jnp.zeros((count,) + blocks[0].shape, blocks[0].dtype)
    for block, spot in zip(blocks, spots):
        out = lax.dynamic_update_index_in_dim(out, block, spot, 0)
    return out


class Wires:
    def __init__(self, dp, section):
        assert section == 4 and dp % 2 == 0
        self.dp, self.section = dp, section
        self.depth = dp // 2
        self.hops = self.depth <= 4
        spots = list(itertools.product(range(self.depth), range(2), range(2), range(2)))

        def number(z, x, y, c):
            return (z * 2 + x) * section + y * 2 + c

        def pairs(move):
            return [(number(*spot), number(*move(*spot))) for spot in spots]

        n = self.depth
        self.swap_x = pairs(lambda z, x, y, c: (z, 1 - x, y, c))
        self.swap_y = pairs(lambda z, x, y, c: (z, x, 1 - y, c))
        self.swap_c = pairs(lambda z, x, y, c: (z, x, y, 1 - c))
        self.away_z = [pairs(lambda z, x, y, c, k=k: ((z + k) % n, x, y, c)) for k in range(n)]
        self.away = {
            (k, f): pairs(lambda z, x, y, c, k=k, f=f: ((z + k) % n, (x + f) % 2, y, c))
            for k in range(n)
            for f in range(2)
        }

    def enter(self):
        self.d = lax.axis_index("dp")
        self.s = lax.axis_index("section")
        self.z, self.x = self.d // 2, self.d % 2
        self.y, self.c = self.s // 2, self.s % 2

    def send(self, value, pairs):
        return lax.ppermute(value, AXES, pairs)

    def near_y(self, value):
        return self.send(value, self.swap_y)

    def near_c(self, value):
        return self.send(value, self.swap_c)

    def by_y(self, mine, other, axis):
        return jnp.where(
            self.y == 0,
            jnp.concatenate([mine, other], axis),
            jnp.concatenate([other, mine], axis),
        )

    def by_c(self, mine, other, axis):
        return jnp.where(
            self.c == 0,
            jnp.concatenate([mine, other], axis),
            jnp.concatenate([other, mine], axis),
        )

    def ring(self, k):
        return (self.z + k) % self.depth

    def gather_near(self, block):
        n = self.depth
        return [block] + [self.send(block, self.away_z[n - k]) for k in range(1, n)]

    def gather_far(self, got):
        n = self.depth
        there = [self.send(got[0], self.swap_x)[None], self.send(jnp.stack(got[1:]), self.swap_x)]
        there = jnp.concatenate(there, 0)
        spots = [self.ring(k) * 2 + self.x for k in range(n)]
        spots += [self.ring(k) * 2 + 1 - self.x for k in range(n)]
        return place(got + [there[k] for k in range(n)], spots, self.dp)

    def sum_far(self, blocks, start=0):
        pairs = blocks.reshape((self.depth, 2) + blocks.shape[1:])
        got = self.send(at(pairs, 1 - self.x + start, 1), self.swap_x)
        return at(pairs, self.x, 1), got

    def sum_near(self, mine, got, start=0):
        half = mine.astype(f32) + got.astype(f32)
        low = half.astype(bf16)
        parts = [
            self.send(at(low, self.ring(k) + start), self.away_z[k]) for k in range(1, self.depth)
        ]
        return at(half, self.z), parts

    def gather_rows(self, rows):
        if not self.hops:
            return lax.all_gather(rows, "dp", axis=0, tiled=True)
        n = self.depth
        got = [rows] + [self.send(rows, self.away_z[n - k]) for k in range(1, n)]
        got += [self.send(item, self.swap_x) for item in got]
        return jnp.concatenate(got, 0)

    def row_order(self):
        n = self.depth
        return [self.ring(k) * 2 + (self.x + f) % 2 for f in range(2) for k in range(n)]

    def sum_rows(self, partial):
        if not self.hops:
            return lax.psum_scatter(partial, "dp", scatter_dimension=0, tiled=True)
        n = self.depth
        half = partial.shape[0] // 2
        got = self.send(partial[half:].astype(bf16), self.swap_x)
        near = partial[:half] + got.astype(f32)
        low = near.astype(bf16).reshape((n, half // n) + partial.shape[1:])
        total = near[: half // n]
        for k in range(1, n):
            total = total + self.send(low[k], self.away_z[k]).astype(f32)
        return total

    def trade_near(self, blocks):
        n = self.depth
        got = []
        for k in range(n):
            pair = [blocks(self.ring(k) * 2 + (self.x + f) % 2) for f in range(2)]
            pair = jnp.stack(pair)
            got.append(pair if k == 0 else self.send(pair, self.away_z[k]))
        return got

    def trade_far(self, got, zero):
        far = jnp.stack([at(pair, 1 + zero.index) for pair in got])
        return [at(pair, zero.index) for pair in got], self.send(far, self.swap_x)

    def trade_order(self):
        n = self.depth
        return [self.ring(n - k) * 2 + (self.x + f) % 2 for f in range(2) for k in range(n)]

    def trade_all(self, blocks):
        mine = jnp.stack([blocks(d) for d in range(self.dp)])
        return lax.all_to_all(mine, "dp", 0, 0, tiled=True)

    def spread(self, rows):
        half = rows.shape[2] // 2
        got = self.near_y(cut(rows, half * (1 - self.y), half, 2).astype(bf16)).astype(f32)
        return self.spread_c(self.by_y(cut(rows, half * self.y, half, 2), got, 1))

    def spread_c(self, cols):
        axis = cols.ndim - 1
        half = cols.shape[axis] // 2
        got = self.near_c(cut(cols, half * (1 - self.c), half, axis).astype(bf16))
        mine = cut(cols, half * self.c, half, axis)
        return self.by_c(mine[None], got.astype(cols.dtype)[None], 0)


def expand(value, heads):
    rows, width = value.shape
    size = width // heads
    owner = lax.broadcasted_iota(jnp.int32, (heads, 1, width), 2) // size
    index = lax.broadcasted_iota(jnp.int32, (heads, 1, width), 0)
    return jnp.where(owner == index, value[None], jnp.zeros((), value.dtype)).reshape(
        heads * rows, width
    )


def collapse(value, heads):
    width = value.shape[1]
    size = width // heads
    owner = lax.broadcasted_iota(jnp.int32, (heads, 1, width), 2) // size
    index = lax.broadcasted_iota(jnp.int32, (heads, 1, width), 0)
    return jnp.sum(
        jnp.where(owner == index, value.reshape(heads, -1, width), 0.0), axis=0
    )


def gelu(hidden):
    return jax.nn.gelu(hidden, approximate=False)


def shards(wires):
    def run(
        latents,
        media,
        frames,
        cotangent,
        w_query,
        w_keyval,
        w_output,
        w_inner,
        w_outer,
        norm_gains,
        norm_biases,
    ):
        wires.enter()
        y, c, s = wires.y, wires.c, wires.s
        dp = wires.dp
        layers, shard, width = w_query.shape
        size = width // H
        scale = size ** (-0.5)
        half = width // 2
        media_len = media.shape[1]
        lat_len = latents.shape[1]
        rows = lat_len // 2
        local = H // 4
        quarter = local * size
        group = local * lat_len
        span = w_inner.shape[2] // dp
        part = shard // 4
        top = layers - 1

        column = lax.broadcasted_iota(jnp.int32, (width, quarter), 1)
        row = lax.broadcasted_iota(jnp.int32, (width, quarter), 0)
        wanted = (2 * (local * c + column // size) + y) * size + column % size
        pick = (row == wanted).astype(bf16)
        stacked = jnp.concatenate([w_query, w_keyval[:, :, :width], w_keyval[:, :, width:]], 1)
        picked = dot(stacked.reshape(-1, width), pick).astype(bf16)
        picked = picked.reshape(layers, 3, shard, quarter)
        vectors = jnp.concatenate([norm_gains, norm_biases], 1).reshape(layers * 6, shard)

        def inner_block(level, parts, index, start):
            count = shard // parts

            def block(d):
                at_row = count * index + start
                block = lax.dynamic_slice(w_inner, (level, at_row, span * d), (1, count, span))
                return block[0]

            return block

        def weights_of(whole):
            whole = whole.reshape(-1, whole.shape[2])
            return [whole, wires.near_c(whole)]

        def joined(whole):
            whole = whole.reshape(dp, 2, size, quarter)
            return jnp.concatenate([whole[:, h].reshape(half, quarter) for h in range(2)], 1)[None]

        w_attn = [None] * layers
        if wires.hops:
            out_piece = lax.dynamic_slice(
                w_output, (0, size * y, half * c), (layers, size, half)
            )
            padded = jnp.zeros((128, shard), bf16).at[: layers * 6].set(vectors)
            first = jnp.concatenate([picked[0, 0], picked[0, 1], padded.T], 1)
            first = wires.gather_near(first)
            out_piece = jnp.concatenate([out_piece[..., :quarter], out_piece[..., quarter:]], 1)
            second = lax.all_gather(jnp.stack([picked[0, 2], out_piece[0]]), "dp", axis=1)
            zero, _ = gate(first[1:])
            piece = jnp.concatenate([picked[1], out_piece[1][None]], 0)
            rest = lax.all_gather(later(piece, zero), "dp", axis=1)
            inner0 = wires.trade_near(inner_block(0, 2, c, zero.index))
            first = wires.gather_far(first)
            first = [first[:, :, i * quarter : (i + 1) * quarter] for i in range(2)] + [
                first[:, :, 2 * quarter :]
            ]
            one = lax.broadcasted_iota(jnp.int32, (layers * 6, 128), 0)
            one = (one == lax.broadcasted_iota(jnp.int32, (layers * 6, 128), 1)).astype(bf16)
            vectors = dot_cols(one, first[2].reshape(width, 128))
        else:
            vectors = lax.all_gather(vectors, "dp", axis=1, tiled=True)
        vectors = vectors.astype(f32).reshape(layers, 2, 3, width)
        gains, biases = vectors[:, 0], vectors[:, 1]

        both = jnp.stack([latents, cotangent])
        got = wires.near_c(at(both, 1 - c, 1))
        wide = wires.by_c(at(both, c, 1), got, 2)
        whole = wires.by_y(wide, wires.near_y(wide), 2)
        whole = jnp.where(y == 0, whole, jnp.roll(whole, rows, axis=1))
        state = whole[0].astype(f32)
        target = whole[1, :rows]

        hat_f, rstd_media = normed(at(media, c).astype(f32))
        hat = hat_f.astype(bf16)
        keep = jnp.arange(media_len) < at(frames, c) * (media_len // MAXF)

        def look(lat_norm, w_q, w_k, level):
            gain, bias = gains[level, 0], biases[level, 0]
            query = [dot(lat_norm, w).astype(bf16) for w in w_q]
            query_x = [expand(q, local) for q in query]
            lifted = jnp.concatenate([dot_cols(q, k) for q, k in zip(query_x, w_k)], 0)
            lifted = lifted * scale
            key_g = (lifted * gain).astype(bf16)
            key_l = lifted.astype(bf16)
            shift = jnp.sum(lifted * bias, axis=-1, keepdims=True)
            scores = dot_cols(key_g, hat) + shift
            scores = jnp.where(keep[None], scores, -1e30)
            scores_l = dot_cols(key_l, lat_norm)
            high = jnp.maximum(
                jnp.max(scores, axis=-1, keepdims=True), jnp.max(scores_l, axis=-1, keepdims=True)
            )
            expo, expo_l = jnp.exp(scores - high), jnp.exp(scores_l - high)
            total = jnp.sum(expo, axis=-1, keepdims=True) + jnp.sum(expo_l, axis=-1, keepdims=True)
            low, low_l = (expo / total).astype(bf16), (expo_l / total).astype(bf16)
            mass = jnp.sum(low.astype(f32), axis=-1, keepdims=True)
            mixed_hat = dot(low, hat)
            mixed = (mixed_hat * gain + mass * bias + dot(low_l, lat_norm)).astype(bf16)
            mixed_hat = mixed_hat.astype(bf16)
            return dict(
                query=query, query_x=query_x, key_g=key_g, key_l=key_l,
                low=low, low_l=low_l, mass=mass, mixed_hat=mixed_hat, mixed=mixed,
            )

        def answer(kept, w_v, w_o):
            mixed = kept["mixed"]
            att = [
                collapse(dot(mixed[i * group : (i + 1) * group], v), local).astype(bf16)
                for i, v in enumerate(w_v)
            ]
            attended = wires.by_c(att[0], att[1], 1)
            kept["attended"] = attended
            return wires.by_c(dot(attended, w_o[0]), dot(attended, w_o[1]), 1)

        def answer_back(d_mid, lat_norm, weights, level, kept):
            w_v, w_o = weights[2], weights[3]
            gain, bias = gains[level, 0], biases[level, 0]
            d_mine, d_other = cut(d_mid, half * c, half), cut(d_mid, half * (1 - c), half)
            d_att = (dot_cols(d_mine, w_o[0]) + dot_cols(d_other, w_o[1])).astype(bf16)
            d_att = [cut(d_att, quarter * c, quarter), cut(d_att, quarter * (1 - c), quarter)]
            d_att_x = [expand(v, local) for v in d_att]
            raised = jnp.concatenate([dot_cols(a, v) for a, v in zip(d_att_x, w_v)], 0)
            val_g = (raised * gain).astype(bf16)
            val_l = raised.astype(bf16)
            shift = jnp.sum(raised * bias, axis=-1, keepdims=True)
            kept.update(d_att=d_att, d_att_x=d_att_x, val_g=val_g, val_l=val_l)
            kept.update(shift=shift, d_mine=d_mine, d_other=d_other)

        def look_back(lat_norm, weights, level, kept):
            w_q, w_k = weights[0], weights[1]
            gain, bias = gains[level, 0], biases[level, 0]
            probs, probs_l = kept["low"].astype(f32), kept["low_l"].astype(f32)
            d_probs = dot_cols(kept["val_g"], hat) + kept["shift"]
            d_probs_l = dot_cols(kept["val_l"], lat_norm)
            along = jnp.sum(probs * d_probs, axis=-1, keepdims=True)
            along = along + jnp.sum(probs_l * d_probs_l, axis=-1, keepdims=True)
            ds = (probs * (d_probs - along)).astype(bf16)
            ds_l = (probs_l * (d_probs_l - along)).astype(bf16)
            ds_mass = jnp.sum(ds.astype(f32), axis=-1, keepdims=True)
            ds_hat = dot(ds, hat)
            d_lift = (ds_hat * gain + ds_mass * bias + dot(ds_l, lat_norm)).astype(bf16)
            d_query = [
                (collapse(dot(d_lift[i * group : (i + 1) * group], k), local) * scale).astype(bf16)
                for i, k in enumerate(w_k)
            ]
            d_lat = dot_cols(d_query[0], w_q[0]) + dot_cols(d_query[1], w_q[1])
            d_lat = d_lat + dot_rows(
                jnp.concatenate([ds_l, kept["low_l"]], 0),
                jnp.concatenate([kept["key_l"], kept["val_l"]], 0),
            )
            lifted, raised = kept["key_l"].astype(f32), kept["val_l"].astype(f32)
            d_gain = jnp.sum(lifted * ds_hat + raised * kept["mixed_hat"].astype(f32), axis=0)
            d_bias = jnp.sum(lifted * ds_mass + raised * kept["mass"], axis=0)
            kept.update(ds=ds, d_lift=d_lift, d_query=d_query, d_gain=d_gain, d_bias=d_bias)
            return d_lat

        def value_grads(kept, zero):
            small = [kept["attended"], kept["d_other"], kept["d_att"][1]]
            got = wires.near_c(later(jnp.concatenate(small, 1), zero))
            attended, d_mine, d_att = got[:, :half], got[:, half:width], got[:, width:]
            mixed = wires.near_c(later(kept["mixed"][group:], zero))
            mixed = jnp.concatenate([kept["mixed"][:group], mixed], 0)
            d_att = jnp.concatenate([kept["d_att_x"][0], expand(d_att, local)], 0)
            g_value = dot_rows(mixed, d_att).astype(bf16)
            attended = jnp.concatenate([kept["attended"], attended], 0)
            d_mine = jnp.concatenate([kept["d_mine"], d_mine], 0)
            g_output = dot_rows(attended, d_mine).astype(bf16)
            return [g_value, g_output]

        def query_grads(lat_norm, kept, zero):
            small = [lat_norm, kept["query"][1], kept["d_query"][1]]
            got = wires.near_c(later(jnp.concatenate(small, 1), zero))
            lat, query, d_query = got[:, :width], got[:, width : width + quarter], got[:, width + quarter :]
            lift = wires.near_c(later(kept["d_lift"][group:], zero))
            lift = jnp.concatenate([kept["d_lift"][:group], lift], 0)
            query = jnp.concatenate([kept["query_x"][0], expand(query, local)], 0)
            g_key = (dot_rows(lift, query) * scale).astype(bf16)
            lat = jnp.concatenate([lat_norm, lat], 0)
            d_query = jnp.concatenate([kept["d_query"][0], d_query], 0)
            return [dot_rows(lat, d_query).astype(bf16), g_key]

        index = lax.broadcasted_iota(jnp.int32, (half, half), 0)
        goal = lax.broadcasted_iota(jnp.int32, (half, half), 1)
        head, within = index // size, index % size
        order = ((head % local) * 2 + head // local) * size + within
        shuffle = (order == goal).astype(bf16)

        def columns(v):
            n = v.shape[2]
            both = [jnp.concatenate([v[0, i], v[1, i]], 1) for i in range(2)]
            out = dot(jnp.concatenate(both, 0), shuffle)
            return jnp.concatenate([out[:n], out[n:]], 1)

        def finish(query, key, value, out):
            out = jnp.concatenate([out[:, 0], out[:, 1]], 2).reshape(shard, width).astype(f32)
            key_value = jnp.concatenate([columns(key), columns(value)], 1)
            return columns(query), key_value, out

        def finish_generic(query_key, g_value, g_output):
            blocks = jnp.concatenate(query_key + [g_value], 1).reshape(dp, shard, 3 * quarter)
            parts = lax.psum_scatter(blocks, "dp", scatter_dimension=0, tiled=False)
            whole = g_output.reshape(H // 2, 1, size, half)
            whole = wires.by_y(whole, jnp.zeros_like(whole), 1).reshape(dp, shard, half)
            out = lax.psum_scatter(whole, "dp", scatter_dimension=0, tiled=False)
            parts = lax.all_gather(parts, "section", axis=0).reshape(2, 2, shard, 3 * quarter)
            out = lax.all_gather(out, "section", axis=0).reshape(2, 2, shard, half)
            out = jnp.sum(out.astype(f32), 0)
            parts = [columns(parts[..., j * quarter : (j + 1) * quarter]) for j in range(3)]
            out = jnp.concatenate([out[0], out[1]], 1)
            return parts[0], jnp.concatenate(parts[1:], 1), out

        def ffn_grads(active, dz_all, mn_all, d_hidden):
            g_inner = dot_rows(mn_all, d_hidden).astype(bf16)
            return g_inner, dot_rows(active, dz_all).astype(bf16)

        def norm_latents(x_hat, level):
            return (x_hat * gains[level, 1] + biases[level, 1]).astype(bf16)

        def middle(x_rows, branch, level):
            branch = branch[:rows] + wires.near_y(branch[rows:].astype(bf16)).astype(f32)
            mid = (x_rows + branch).astype(bf16).astype(f32)
            hat_m, rstd_m = normed(mid)
            mn = (hat_m * gains[level, 2] + biases[level, 2]).astype(bf16)
            return mid, hat_m, rstd_m, mn

        def ffn_back(dz_all, hidden, level):
            d_active = dot_cols(dz_all, w_outer[level])
            return jax.vjp(gelu, hidden)[1](d_active)[0].astype(bf16)

        def middle_back(grad, hat_m, rstd_m, d_mn, level):
            d_low = (grad + norm_back(hat_m, rstd_m, d_mn * gains[level, 2])).astype(bf16)
            return d_low, jnp.concatenate([d_low, wires.near_y(d_low)], 0)

        def latents_back(d_low, d_lat, x_hat, x_rstd, level):
            d_norm = d_lat[:rows] + wires.near_y(d_lat[rows:].astype(bf16)).astype(f32)
            grad = d_low.astype(f32) + norm_back(x_hat, x_rstd, d_norm * gains[level, 1])
            if level > 0:
                grad = grad.astype(bf16).astype(f32)
            return d_norm, grad

        def vector_rows(attn, d_norm, x_hat, d_mn, hat_m):
            return [
                attn["d_gain"],
                jnp.sum(d_norm * x_hat, 0),
                jnp.sum(d_mn * hat_m, 0),
                attn["d_bias"],
                jnp.sum(d_norm, 0),
                jnp.sum(d_mn, 0),
            ]

        def media_pair(attn):
            left = jnp.concatenate([attn["ds"], attn["low"]], 0)
            return left, jnp.concatenate([attn["key_g"], attn["val_g"]], 0)

        def outputs(x_low, grad, media_grad, outs, sums):
            sums = sums.reshape(layers, 2, 3, shard)
            both = wires.spread(jnp.stack([x_low.astype(f32), grad]))
            return (
                both[:, 0].astype(bf16),
                media_grad,
                both[:, 1],
                *outs,
                sums[:, 0, :2],
                sums[:, 1, :2],
                sums[:, :, 2],
            )

        x_hat0, x_rstd0 = normed(state)
        lat_norm0 = norm_latents(x_hat0, 0)
        x_hat0, x_rstd0 = x_hat0[:rows], x_rstd0[:rows]
        x_rows0 = state[:rows]

        if not wires.hops:
            nil = Zero(jnp.zeros((1, 1), f32), 0)
            x_rows, x_hat, x_rstd, lat_norm = x_rows0, x_hat0, x_rstd0, lat_norm0
            kept = []
            for level in range(layers):
                got = [
                    lax.all_gather(picked[level, j], "dp", axis=0).reshape(width, quarter)
                    for j in range(3)
                ]
                out = lax.all_gather(w_output[level], "dp", axis=0, tiled=True)
                out = at(out.reshape(H // 2, 2, size, 2, half), y, 1)
                got.append(at(out, c, 2).reshape(half, half))
                weights = [[item, wires.near_c(item)] for item in got]
                w_in = wires.trade_all(inner_block(level, 1, 0, 0)).reshape(width, span)
                if level > 0:
                    x_hat, x_rstd = normed(x_rows)
                    mine = norm_latents(x_hat, level)
                    lat_norm = jnp.concatenate([mine, wires.near_y(mine)], 0)
                attn = look(lat_norm, weights[0], weights[1], level)
                branch = answer(attn, weights[2], weights[3])
                mid, hat_m, rstd_m, mn = middle(x_rows, branch, level)
                mn_all = wires.gather_rows(mn)
                hidden = dot(mn_all, w_in)
                active = gelu(hidden).astype(bf16)
                x_low = (mid + wires.sum_rows(dot(active, w_outer[level]))).astype(bf16)
                x_rows = x_low.astype(f32)
                kept.append(
                    (attn, lat_norm, x_hat, x_rstd, hat_m, rstd_m, mn_all, hidden, active, weights, w_in)
                )
            grad = target.astype(f32)
            ffn_out, attn_out, vector_grads, media_sum = [], [], [], 0.0
            for level in reversed(range(layers)):
                attn, lat_norm, x_hat, x_rstd, hat_m, rstd_m, mn_all, hidden, active, weights, w_in = kept[level]
                dz_all = wires.gather_rows(grad.astype(bf16))
                d_hidden = ffn_back(dz_all, hidden, level)
                d_mn = wires.sum_rows(dot_cols(d_hidden, w_in))
                share = ffn_grads(active, dz_all, mn_all, d_hidden)
                share = [lax.psum(v.astype(f32), "section") for v in share]
                inner = share[0].reshape(dp, shard, span).astype(bf16)
                inner = wires.trade_all(lambda d: inner[d])
                inner = jnp.transpose(inner, (1, 0, 2)).reshape(shard, dp * span)
                ffn_out.insert(0, (inner.astype(f32), share[1]))
                d_low, d_mid = middle_back(grad, hat_m, rstd_m, d_mn, level)
                answer_back(d_mid, lat_norm, weights, level, attn)
                d_lat = look_back(lat_norm, weights, level, attn)
                d_norm, grad = latents_back(d_low, d_lat, x_hat, x_rstd, level)
                vector_grads = vector_rows(attn, d_norm, x_hat, d_mn, hat_m) + vector_grads
                attn_out.insert(
                    0, finish_generic(query_grads(lat_norm, attn, nil), *value_grads(attn, nil))
                )
                media_sum = media_sum + dot_rows(*media_pair(attn))
            d_media = norm_back(hat.astype(f32), rstd_media, media_sum)
            got = wires.near_y(cut(d_media, half * (1 - y), half).astype(bf16))
            media_grad = wires.spread_c(cut(d_media, half * y, half) + got.astype(f32))
            extra = lax.psum(jnp.stack(vector_grads), "section")
            sums = lax.psum_scatter(extra, "dp", scatter_dimension=1, tiled=True)
            outs = [jnp.stack([attn_out[level][i] for level in range(layers)]) for i in range(3)]
            outs += [jnp.stack([ffn_out[level][i] for level in range(layers)]) for i in range(2)]
            return outputs(x_low, grad, media_grad, outs, sums)

        order = wires.trade_order()
        w_q, w_k = [weights_of(v) for v in first[:2]]
        attn0 = look(lat_norm0, w_q, w_k, 0)
        zero, (second,) = gate([attn0["low"]], [second])
        inner0 = wires.trade_far(inner0, zero)
        w_v, w_o = [weights_of(v) for v in (second[0], joined(second[1]))]
        weights0 = [w_q, w_k, w_v, w_o]
        branch = answer(attn0, w_v, w_o)
        zero, (branch,) = gate([inner0[1]], [branch])
        step = zero.index
        mid0, hat_m0, rstd_m0, mn = middle(x_rows0, branch, 0)
        mn_all0 = wires.gather_rows(mn)
        inner0 = place(inner0[0] + list(inner0[1]), [v + step for v in order], dp)
        inner0 = wires.by_c(inner0[:, None], wires.near_c(inner0)[:, None], 1)
        w_in0 = inner0.reshape(width, span)
        hidden0 = dot(mn_all0, w_in0)
        active0 = gelu(hidden0).astype(bf16)
        x_low = (mid0 + wires.sum_rows(dot(active0, w_outer[0]))).astype(bf16)

        zero, (x_low, rest) = gate([], [x_low, rest])
        inner1 = wires.trade_near(inner_block(1, 4, s, zero.index))
        targets = wires.gather_near(later(target, zero))
        x_rows1 = x_low.astype(f32)
        x_hat1, x_rstd1 = normed(x_rows1)
        mine = norm_latents(x_hat1, 1)
        lat_norm1 = jnp.concatenate([mine, wires.near_y(mine)], 0)
        weights1 = [weights_of(v) for v in (rest[0], rest[1], rest[2], joined(rest[3]))]
        attn1 = look(lat_norm1, weights1[0], weights1[1], 1)
        zero, _ = gate([attn1["low"]])
        inner1 = wires.trade_far(inner1, zero)
        targets = later(jnp.concatenate(targets, 0), zero)
        target_all = jnp.concatenate([targets, wires.send(targets, wires.swap_x)], 0)
        branch = answer(attn1, weights1[2], weights1[3])
        zero, (branch,) = gate([], [branch])
        step = zero.index
        mid1, hat_m1, rstd_m1, mn = middle(x_rows1, branch, 1)
        mn_all1 = wires.gather_rows(mn)
        inner1 = place(inner1[0] + list(inner1[1]), [v + step for v in order], dp)
        inner1 = wires.by_y(inner1[:, None], wires.near_y(inner1)[:, None], 1)
        inner1 = wires.by_c(inner1[:, :, None], wires.near_c(inner1)[:, :, None], 2)
        w_in1 = inner1.reshape(width, span)
        hidden1 = dot(mn_all1, w_in1)
        active1 = gelu(hidden1).astype(bf16)
        x_part = dot(active1, w_outer[1]).astype(bf16)

        d_hidden = ffn_back(target_all, hidden1, 1)
        d_mn1 = wires.sum_rows(dot_cols(d_hidden, w_in1))
        g_ffn = ffn_grads(active1, target_all, mn_all1, d_hidden)
        zero, (d_mn1,) = gate(g_ffn, [d_mn1])

        def shared(grads):
            g_inner = jnp.transpose(grads[0].reshape(dp, 4, part, span), (1, 0, 2, 3))
            parts = [g_inner, grads[1].reshape(4, span // 4, width)]
            return [lax.psum_scatter(v, "section", scatter_dimension=0) for v in parts]

        def output_blocks(grad):
            grad = grad.reshape(dp, size, half)
            return jnp.concatenate([grad[:, :, :quarter], grad[:, :, quarter:]], 1)

        def output_columns(v):
            v = v.reshape(2, 2, 2, size, quarter)
            return jnp.concatenate([v[:, :, 0], v[:, :, 1]], 3)

        share1 = shared(g_ffn)
        d_low1, d_mid1 = middle_back(target.astype(f32), hat_m1, rstd_m1, d_mn1, 1)
        answer_back(d_mid1, lat_norm1, weights1, 1, attn1)
        d_lat = look_back(lat_norm1, weights1, 1, attn1)
        zero, (d_lat,) = gate([], [d_lat])
        d_norm1, grad = latents_back(d_low1, d_lat, x_hat1, x_rstd1, 1)
        dz_all = wires.gather_rows(grad.astype(bf16))
        g_attn = query_grads(lat_norm1, attn1, zero) + value_grads(attn1, zero)

        zero, (dz_all,) = gate(g_attn, [dz_all])
        blocks = [v.reshape(dp, shard, quarter) for v in g_attn[:3]] + [output_blocks(g_attn[3])]
        blocks = jnp.concatenate(blocks, 2)
        blocks1 = lax.psum_scatter(blocks, "dp", scatter_dimension=0, tiled=False)
        d_hidden = ffn_back(dz_all, hidden0, 0)
        d_mn0 = wires.sum_rows(dot_cols(d_hidden, w_in0))
        g_ffn = ffn_grads(active0, dz_all, mn_all0, d_hidden)
        left, right = media_pair(attn1)
        media_sum = dot_rows(left, later(right, zero))
        zero, (d_mn0, *g_ffn) = gate([media_sum, *share1], [d_mn0, *g_ffn])
        share0 = shared(g_ffn)
        d_low0, d_mid0 = middle_back(grad, hat_m0, rstd_m0, d_mn0, 0)
        answer_back(d_mid0, lat_norm0, weights0, 0, attn0)
        g_vo = value_grads(attn0, zero)
        zero, (attn0["shift"],) = gate(g_vo, [attn0["shift"]])
        g_vo = jnp.concatenate([g_vo[0].reshape(dp, shard, quarter), output_blocks(g_vo[1])], 2)
        g_vo = wires.sum_far(g_vo, zero.index)
        d_lat = look_back(lat_norm0, weights0, 0, attn0)
        zero, (d_lat, attn0["d_lift"]) = gate([], [d_lat, attn0["d_lift"]])
        d_norm0, grad = latents_back(d_low0, d_lat, x_hat0, x_rstd0, 0)
        left, right = media_pair(attn0)
        media_sum = media_sum + dot_rows(left, later(right, zero))
        d_media = norm_back(hat.astype(f32), rstd_media, media_sum)
        send = cut(d_media, half * (1 - y), half).astype(bf16)
        zero, (send, grad, attn0["d_lift"]) = gate([g_vo[1]], [send, grad, attn0["d_lift"]])
        got = wires.near_y(send)
        g_vo = wires.sum_near(g_vo[0], later(g_vo[1], zero))
        x_part = wires.sum_rows(later(x_part, zero).astype(f32))
        extra = vector_rows(attn0, d_norm0, x_hat0, d_mn0, hat_m0)
        extra += vector_rows(attn1, d_norm1, x_hat1, d_mn1, hat_m1)
        extra = jnp.zeros((128, width), f32).at[: layers * 6].set(jnp.stack(extra)).T
        g_qk = query_grads(lat_norm0, attn0, zero) + [extra.astype(bf16)]
        g_qk = jnp.concatenate(g_qk, 1)
        zero, (g_qk, blocks1, *share1) = gate([], [g_qk, blocks1, *share1])
        step = zero.index
        g_qk = wires.sum_far(g_qk.reshape(dp, shard, g_qk.shape[1]), step)
        blocks1 = lax.all_gather(blocks1, "section", axis=0)
        outer1 = lax.all_gather(share1[1], "section", axis=0, tiled=True)
        zero, (far, grad, share0[0]) = gate([*g_vo[1], x_part], [g_qk[1], grad, share0[0]])
        step = zero.index
        g_qk = wires.sum_near(g_qk[0], far)
        blocks1 = later(blocks1, zero).reshape(2, 2, shard, 4 * quarter)
        parts = [blocks1[..., j * quarter : (j + 1) * quarter] for j in range(4)]
        attn_out1 = finish(*parts[:3], output_columns(parts[3]))
        zero, (outer0,) = gate(attn_out1, [share0[1]])
        outer0 = lax.all_gather(outer0, "section", axis=0, tiled=True)
        step = zero.index
        trade = jnp.concatenate([share1[0], share0[0]], 1)
        trade = wires.trade_near(lambda d: at(trade, d + step))
        outs = [jnp.zeros((layers,) + v.shape, f32).at[1].set(v) for v in attn_out1]
        zero, (grad, *arrived) = gate([], [grad, *g_qk[1], *outs])
        arrived, outs = arrived[:-3], arrived[-3:]
        g_qk = (g_qk[0], arrived)
        trade = wires.trade_far(trade, zero)
        x_out = (mid1 + x_part + zero.value).astype(bf16)

        def summed(mine, parts):
            for v in parts:
                mine = mine + v.astype(f32)
            return mine.astype(bf16)

        four = jnp.concatenate([summed(*g_vo), summed(*g_qk)], 1)
        four_y = wires.near_y(four)
        inner = []
        for i in range(layers):
            rows_of = slice(i * part, (i + 1) * part)
            inner.append(line_up([v[rows_of] for v in trade[0] + list(trade[1])], order))
        inner = jnp.stack(inner)
        zero, _ = gate([inner])
        inner = lax.all_gather(inner, "section", axis=0)
        four = wires.by_y(four[None], later(four_y, zero)[None], 0)
        four = wires.by_c(four[:, None], wires.near_c(four)[:, None], 1)
        value, out, query, key = [four[..., i * quarter : (i + 1) * quarter] for i in range(4)]
        sums = jnp.sum(four[..., 4 * quarter :].astype(f32), axis=(0, 1))[:, : layers * 6].T
        inner = [inner[:, i].reshape(shard, dp * span).astype(f32) for i in range(layers)]
        ffn_out = [(inner[1], outer0.astype(f32)), (inner[0], outer1.astype(f32))]
        attn_out0 = finish(query, key, value, output_columns(out))
        media_grad = wires.spread_c(cut(d_media, half * y, half) + later(got, zero).astype(f32))
        outs = [v.at[0].set(u) for v, u in zip(outs, attn_out0)]
        outs += [jnp.stack([ffn_out[level][i] for level in range(layers)]) for i in range(2)]
        return outputs(x_out, grad, media_grad, outs, sums)

    return run


def solution(mesh):
    wires = Wires(mesh.shape["dp"], mesh.shape["section"])
    return jax.shard_map(
        shards(wires),
        mesh=mesh,
        in_specs=(
            P("dp", None, "section"),
            P("dp", None, None),
            P("dp"),
            P("dp", None, "section"),
            P(None, "dp", None),
            P(None, "dp", None),
            P(None, "dp", None),
            P(None, "dp", None),
            P(None, "dp", None),
            P(None, None, "dp"),
            P(None, None, "dp"),
        ),
        out_specs=(
            P("dp", None, "section"),
            P("dp", None, "section"),
            P("dp", None, "section"),
            P(None, "dp", None),
            P(None, "dp", None),
            P(None, "dp", None),
            P(None, "dp", None),
            P(None, "dp", None),
            P(None, None, "dp"),
            P(None, None, "dp"),
            P(None, None, "dp"),
        ),
        check_vma=False,
    )
```

```python
import itertools

import jax
import jax.numpy as jnp
from jax import lax
from jax.experimental import pallas as pl
from jax.experimental.pallas import tpu as pltpu
from jax.sharding import PartitionSpec as P

H = 16
MAXF = 8
eps = 1e-05
bf16 = jnp.bfloat16
f32 = jnp.float32
AXES = ("dp", "section")


def dot(left, right):
    return jnp.dot(left, right, preferred_element_type=f32)


def dot_rows(left, right):
    return lax.dot_general(left, right, (((0,), (0,)), ((), ())), preferred_element_type=f32)


def dot_cols(left, right):
    return lax.dot_general(left, right, (((1,), (1,)), ((), ())), preferred_element_type=f32)


def at(array, index, axis=0):
    return lax.dynamic_index_in_dim(array, index, axis, keepdims=False)


def normed(value):
    centred = value - jnp.mean(value, axis=-1, keepdims=True)
    spread = jnp.mean(centred * centred, axis=-1, keepdims=True)
    rstd = lax.rsqrt(spread + eps)
    return centred * rstd, rstd


def norm_back(hat, rstd, grad):
    mean = jnp.mean(grad, axis=-1, keepdims=True)
    along = jnp.mean(grad * hat, axis=-1, keepdims=True)
    return rstd * (grad - mean - hat * along)


class Zero:
    def __init__(self, value, index):
        self.value, self.index = value, index


def gate(needed, carried=()):
    needed, carried = list(needed), list(carried)
    count = len(needed) + len(carried)

    def kernel(*refs):
        refs[count][...] = jnp.zeros((1, 1), f32)
        refs[count + 1][0, 0] = jnp.int32(0)

    anywhere = pl.BlockSpec(memory_space=pl.ANY)
    out = pl.pallas_call(
        kernel,
        out_shape=[jax.ShapeDtypeStruct((1, 1), f32), jax.ShapeDtypeStruct((1, 1), jnp.int32)]
        + [jax.ShapeDtypeStruct(v.shape, v.dtype) for v in carried],
        in_specs=[anywhere] * count,
        out_specs=[
            pl.BlockSpec(memory_space=pltpu.VMEM),
            pl.BlockSpec(memory_space=pltpu.SMEM),
        ]
        + [anywhere] * len(carried),
        input_output_aliases={len(needed) + i: i + 2 for i in range(len(carried))},
    )(*needed, *carried)
    return Zero(out[0], out[1].reshape(())), list(out[2:])


def later(value, zero):
    return value + zero.value.astype(value.dtype).reshape((1,) * value.ndim)


def line_up(blocks, order):
    rows, lanes = blocks[0].shape
    count = len(blocks)

    def kernel(order_ref, *refs):
        out = refs[-1]
        for i in range(count):
            spot = pl.multiple_of(order_ref[i] * lanes, lanes)
            out[:, pl.ds(spot, lanes)] = refs[i][...]

    return pl.pallas_call(
        kernel,
        out_shape=jax.ShapeDtypeStruct((rows, count * lanes), blocks[0].dtype),
        in_specs=[pl.BlockSpec(memory_space=pltpu.SMEM)]
        + [pl.BlockSpec(memory_space=pltpu.VMEM)] * count,
        out_specs=pl.BlockSpec(memory_space=pltpu.VMEM),
    )(jnp.stack(order).astype(jnp.int32), *blocks)


def cut(array, start, size, axis=1):
    return lax.dynamic_slice_in_dim(array, start, size, axis)


def place(blocks, spots, count):
    out = jnp.zeros((count,) + blocks[0].shape, blocks[0].dtype)
    for block, spot in zip(blocks, spots):
        out = lax.dynamic_update_index_in_dim(out, block, spot, 0)
    return out


class Wires:
    def __init__(self, dp, section):
        assert section == 4 and dp % 2 == 0
        self.dp, self.section = dp, section
        self.depth = dp // 2
        self.hops = self.depth <= 4
        spots = list(itertools.product(range(self.depth), range(2), range(2), range(2)))

        def number(z, x, y, c):
            return (z * 2 + x) * section + y * 2 + c

        def pairs(move):
            return [(number(*spot), number(*move(*spot))) for spot in spots]

        n = self.depth
        self.swap_x = pairs(lambda z, x, y, c: (z, 1 - x, y, c))
        self.swap_y = pairs(lambda z, x, y, c: (z, x, 1 - y, c))
        self.swap_c = pairs(lambda z, x, y, c: (z, x, y, 1 - c))
        self.away_z = [pairs(lambda z, x, y, c, k=k: ((z + k) % n, x, y, c)) for k in range(n)]
        self.away = {
            (k, f): pairs(lambda z, x, y, c, k=k, f=f: ((z + k) % n, (x + f) % 2, y, c))
            for k in range(n)
            for f in range(2)
        }

    def enter(self):
        self.d = lax.axis_index("dp")
        self.s = lax.axis_index("section")
        self.z, self.x = self.d // 2, self.d % 2
        self.y, self.c = self.s // 2, self.s % 2

    def send(self, value, pairs):
        return lax.ppermute(value, AXES, pairs)

    def near_y(self, value):
        return self.send(value, self.swap_y)

    def near_c(self, value):
        return self.send(value, self.swap_c)

    def by_y(self, mine, other, axis):
        return jnp.where(
            self.y == 0,
            jnp.concatenate([mine, other], axis),
            jnp.concatenate([other, mine], axis),
        )

    def by_c(self, mine, other, axis):
        return jnp.where(
            self.c == 0,
            jnp.concatenate([mine, other], axis),
            jnp.concatenate([other, mine], axis),
        )

    def ring(self, k):
        return (self.z + k) % self.depth

    def gather_near(self, block):
        n = self.depth
        return [block] + [self.send(block, self.away_z[n - k]) for k in range(1, n)]

    def gather_far(self, got):
        n = self.depth
        there = [self.send(got[0], self.swap_x)[None], self.send(jnp.stack(got[1:]), self.swap_x)]
        there = jnp.concatenate(there, 0)
        spots = [self.ring(k) * 2 + self.x for k in range(n)]
        spots += [self.ring(k) * 2 + 1 - self.x for k in range(n)]
        return place(got + [there[k] for k in range(n)], spots, self.dp)

    def sum_far(self, blocks, start=0):
        pairs = blocks.reshape((self.depth, 2) + blocks.shape[1:])
        got = self.send(at(pairs, 1 - self.x + start, 1), self.swap_x)
        return at(pairs, self.x, 1), got

    def sum_near(self, mine, got, start=0):
        half = mine.astype(f32) + got.astype(f32)
        low = half.astype(bf16)
        parts = [
            self.send(at(low, self.ring(k) + start), self.away_z[k]) for k in range(1, self.depth)
        ]
        return at(half, self.z), parts

    def gather_rows(self, rows):
        if not self.hops:
            return lax.all_gather(rows, "dp", axis=0, tiled=True)
        n = self.depth
        got = [rows] + [self.send(rows, self.away_z[n - k]) for k in range(1, n)]
        got += [self.send(item, self.swap_x) for item in got]
        return jnp.concatenate(got, 0)

    def row_order(self):
        n = self.depth
        return [self.ring(k) * 2 + (self.x + f) % 2 for f in range(2) for k in range(n)]

    def sum_rows(self, partial):
        if not self.hops:
            return lax.psum_scatter(partial, "dp", scatter_dimension=0, tiled=True)
        n = self.depth
        half = partial.shape[0] // 2
        partial = partial.astype(bf16)
        got = self.send(partial[half:], self.swap_x)
        near = partial[:half].astype(f32) + got.astype(f32)
        low = near.astype(bf16).reshape((n, half // n) + partial.shape[1:])
        total = near[: half // n]
        for k in range(1, n):
            total = total + self.send(low[k], self.away_z[k]).astype(f32)
        return total

    def trade_near(self, blocks):
        n = self.depth
        got = []
        for k in range(n):
            pair = [blocks(self.ring(k) * 2 + (self.x + f) % 2) for f in range(2)]
            pair = jnp.stack(pair)
            got.append(pair if k == 0 else self.send(pair, self.away_z[k]))
        return got

    def trade_far(self, got, zero):
        far = jnp.stack([at(pair, 1 + zero.index) for pair in got])
        return [at(pair, zero.index) for pair in got], self.send(far, self.swap_x)

    def trade_order(self):
        n = self.depth
        return [self.ring(n - k) * 2 + (self.x + f) % 2 for f in range(2) for k in range(n)]

    def trade_all(self, blocks):
        mine = jnp.stack([blocks(d) for d in range(self.dp)])
        return lax.all_to_all(mine, "dp", 0, 0, tiled=True)

    def spread(self, rows):
        half = rows.shape[2] // 2
        got = self.near_y(cut(rows, half * (1 - self.y), half, 2).astype(bf16)).astype(f32)
        return self.spread_c(self.by_y(cut(rows, half * self.y, half, 2), got, 1))

    def spread_c(self, cols):
        axis = cols.ndim - 1
        half = cols.shape[axis] // 2
        got = self.near_c(cut(cols, half * (1 - self.c), half, axis).astype(bf16))
        mine = cut(cols, half * self.c, half, axis)
        return self.by_c(mine[None], got.astype(cols.dtype)[None], 0)


def expand(value, heads):
    rows, width = value.shape
    size = width // heads
    owner = lax.broadcasted_iota(jnp.int32, (heads, 1, width), 2) // size
    index = lax.broadcasted_iota(jnp.int32, (heads, 1, width), 0)
    return jnp.where(owner == index, value[None], jnp.zeros((), value.dtype)).reshape(
        heads * rows, width
    )


def collapse(value, heads):
    width = value.shape[1]
    size = width // heads
    owner = lax.broadcasted_iota(jnp.int32, (heads, 1, width), 2) // size
    index = lax.broadcasted_iota(jnp.int32, (heads, 1, width), 0)
    return jnp.sum(
        jnp.where(owner == index, value.reshape(heads, -1, width), 0.0), axis=0
    )


def gelu(hidden):
    return jax.nn.gelu(hidden, approximate=False)


def shards(wires):
    def run(
        latents,
        media,
        frames,
        cotangent,
        w_query,
        w_keyval,
        w_output,
        w_inner,
        w_outer,
        norm_gains,
        norm_biases,
    ):
        wires.enter()
        y, c, s = wires.y, wires.c, wires.s
        dp = wires.dp
        layers, shard, width = w_query.shape
        size = width // H
        scale = size ** (-0.5)
        half = width // 2
        media_len = media.shape[1]
        lat_len = latents.shape[1]
        rows = lat_len // 2
        local = H // 4
        quarter = local * size
        group = local * lat_len
        span = w_inner.shape[2] // dp
        part = shard // 4
        top = layers - 1

        column = lax.broadcasted_iota(jnp.int32, (width, quarter), 1)
        row = lax.broadcasted_iota(jnp.int32, (width, quarter), 0)
        wanted = (2 * (local * c + column // size) + y) * size + column % size
        pick = (row == wanted).astype(bf16)
        stacked = jnp.concatenate([w_query, w_keyval[:, :, :width], w_keyval[:, :, width:]], 1)
        picked = dot(stacked.reshape(-1, width), pick).astype(bf16)
        picked = picked.reshape(layers, 3, shard, quarter)
        vectors = jnp.concatenate([norm_gains, norm_biases], 1).reshape(layers * 6, shard)

        def inner_block(level, parts, index, start):
            count = shard // parts

            def block(d):
                at_row = count * index + start
                block = lax.dynamic_slice(w_inner, (level, at_row, span * d), (1, count, span))
                return block[0]

            return block

        def weights_of(whole):
            whole = whole.reshape(-1, whole.shape[2])
            return [whole, wires.near_c(whole)]

        def joined(whole):
            whole = whole.reshape(dp, 2, size, quarter)
            return jnp.concatenate([whole[:, h].reshape(half, quarter) for h in range(2)], 1)[None]

        w_attn = [None] * layers
        if wires.hops:
            out_piece = lax.dynamic_slice(
                w_output, (0, size * y, half * c), (layers, size, half)
            )
            padded = jnp.zeros((128, shard), bf16).at[: layers * 6].set(vectors)
            first = jnp.concatenate([picked[0, 0], picked[0, 1], padded.T], 1)
            first = wires.gather_near(first)
            out_piece = jnp.concatenate([out_piece[..., :quarter], out_piece[..., quarter:]], 1)
            second = lax.all_gather(jnp.stack([picked[0, 2], out_piece[0]]), "dp", axis=1)
            zero, _ = gate(first[1:])
            piece = jnp.concatenate([picked[1], out_piece[1][None]], 0)
            rest = lax.all_gather(later(piece, zero), "dp", axis=1)
            inner0 = wires.trade_near(inner_block(0, 2, c, zero.index))
            first = wires.gather_far(first)
            first = [first[:, :, i * quarter : (i + 1) * quarter] for i in range(2)] + [
                first[:, :, 2 * quarter :]
            ]
            one = lax.broadcasted_iota(jnp.int32, (layers * 6, 128), 0)
            one = (one == lax.broadcasted_iota(jnp.int32, (layers * 6, 128), 1)).astype(bf16)
            vectors = dot_cols(one, first[2].reshape(width, 128))
        else:
            vectors = lax.all_gather(vectors, "dp", axis=1, tiled=True)
        vectors = vectors.astype(f32).reshape(layers, 2, 3, width)
        gains, biases = vectors[:, 0], vectors[:, 1]

        both = jnp.stack([latents, cotangent])
        got = wires.near_c(at(both, 1 - c, 1))
        wide = wires.by_c(at(both, c, 1), got, 2)
        whole = wires.by_y(wide, wires.near_y(wide), 2)
        whole = jnp.where(y == 0, whole, jnp.roll(whole, rows, axis=1))
        state = whole[0].astype(f32)
        target = whole[1, :rows]

        hat_f, rstd_media = normed(at(media, c).astype(f32))
        hat = hat_f.astype(bf16)
        keep = jnp.arange(media_len) < at(frames, c) * (media_len // MAXF)

        def look(lat_norm, w_q, w_k, level):
            gain, bias = gains[level, 0], biases[level, 0]
            query = [dot(lat_norm, w).astype(bf16) for w in w_q]
            query_x = [expand(q, local) for q in query]
            lifted = jnp.concatenate([dot_cols(q, k) for q, k in zip(query_x, w_k)], 0)
            lifted = lifted * scale
            key_g = (lifted * gain).astype(bf16)
            key_l = lifted.astype(bf16)
            shift = jnp.sum(lifted * bias, axis=-1, keepdims=True)
            scores = dot_cols(key_g, hat) + shift
            scores = jnp.where(keep[None], scores, -1e30)
            scores_l = dot_cols(key_l, lat_norm)
            high = jnp.maximum(
                jnp.max(scores, axis=-1, keepdims=True), jnp.max(scores_l, axis=-1, keepdims=True)
            )
            expo, expo_l = jnp.exp(scores - high), jnp.exp(scores_l - high)
            total = jnp.sum(expo, axis=-1, keepdims=True) + jnp.sum(expo_l, axis=-1, keepdims=True)
            low, low_l = (expo / total).astype(bf16), (expo_l / total).astype(bf16)
            mass = jnp.sum(low.astype(f32), axis=-1, keepdims=True)
            mixed_hat = dot(low, hat)
            mixed = (mixed_hat * gain + mass * bias + dot(low_l, lat_norm)).astype(bf16)
            mixed_hat = mixed_hat.astype(bf16)
            return dict(
                query=query, query_x=query_x, key_g=key_g, key_l=key_l,
                low=low, low_l=low_l, mass=mass, mixed_hat=mixed_hat, mixed=mixed,
            )

        def answer(kept, w_v, w_o):
            mixed = kept["mixed"]
            att = [
                collapse(dot(mixed[i * group : (i + 1) * group], v), local).astype(bf16)
                for i, v in enumerate(w_v)
            ]
            attended = wires.by_c(att[0], att[1], 1)
            kept["attended"] = attended
            return wires.by_c(dot(attended, w_o[0]), dot(attended, w_o[1]), 1)

        def answer_back(d_mid, lat_norm, weights, level, kept):
            w_v, w_o = weights[2], weights[3]
            gain, bias = gains[level, 0], biases[level, 0]
            d_mine, d_other = cut(d_mid, half * c, half), cut(d_mid, half * (1 - c), half)
            d_att = (dot_cols(d_mine, w_o[0]) + dot_cols(d_other, w_o[1])).astype(bf16)
            d_att = [cut(d_att, quarter * c, quarter), cut(d_att, quarter * (1 - c), quarter)]
            d_att_x = [expand(v, local) for v in d_att]
            raised = jnp.concatenate([dot_cols(a, v) for a, v in zip(d_att_x, w_v)], 0)
            val_g = (raised * gain).astype(bf16)
            val_l = raised.astype(bf16)
            shift = jnp.sum(raised * bias, axis=-1, keepdims=True)
            kept.update(d_att=d_att, d_att_x=d_att_x, val_g=val_g, val_l=val_l)
            kept.update(shift=shift, d_mine=d_mine, d_other=d_other)

        def look_back(lat_norm, weights, level, kept):
            w_q, w_k = weights[0], weights[1]
            gain, bias = gains[level, 0], biases[level, 0]
            probs, probs_l = kept["low"].astype(f32), kept["low_l"].astype(f32)
            d_probs = dot_cols(kept["val_g"], hat) + kept["shift"]
            d_probs_l = dot_cols(kept["val_l"], lat_norm)
            along = jnp.sum(probs * d_probs, axis=-1, keepdims=True)
            along = along + jnp.sum(probs_l * d_probs_l, axis=-1, keepdims=True)
            ds = (probs * (d_probs - along)).astype(bf16)
            ds_l = (probs_l * (d_probs_l - along)).astype(bf16)
            ds_mass = jnp.sum(ds.astype(f32), axis=-1, keepdims=True)
            ds_hat = dot(ds, hat)
            d_lift = (ds_hat * gain + ds_mass * bias + dot(ds_l, lat_norm)).astype(bf16)
            d_query = [
                (collapse(dot(d_lift[i * group : (i + 1) * group], k), local) * scale).astype(bf16)
                for i, k in enumerate(w_k)
            ]
            d_lat = dot_cols(d_query[0], w_q[0]) + dot_cols(d_query[1], w_q[1])
            d_lat = d_lat + dot_rows(
                jnp.concatenate([ds_l, kept["low_l"]], 0),
                jnp.concatenate([kept["key_l"], kept["val_l"]], 0),
            )
            lifted, raised = kept["key_l"].astype(f32), kept["val_l"].astype(f32)
            d_gain = jnp.sum(lifted * ds_hat + raised * kept["mixed_hat"].astype(f32), axis=0)
            d_bias = jnp.sum(lifted * ds_mass + raised * kept["mass"], axis=0)
            kept.update(ds=ds, d_lift=d_lift, d_query=d_query, d_gain=d_gain, d_bias=d_bias)
            return d_lat

        def value_grads(kept, zero):
            small = [kept["attended"], kept["d_other"], kept["d_att"][1]]
            got = wires.near_c(later(jnp.concatenate(small, 1), zero))
            attended, d_mine, d_att = got[:, :half], got[:, half:width], got[:, width:]
            mixed = wires.near_c(later(kept["mixed"][group:], zero))
            mixed = jnp.concatenate([kept["mixed"][:group], mixed], 0)
            d_att = jnp.concatenate([kept["d_att_x"][0], expand(d_att, local)], 0)
            g_value = dot_rows(mixed, d_att).astype(bf16)
            attended = jnp.concatenate([kept["attended"], attended], 0)
            d_mine = jnp.concatenate([kept["d_mine"], d_mine], 0)
            g_output = dot_rows(attended, d_mine).astype(bf16)
            return [g_value, g_output]

        def query_grads(lat_norm, kept, zero):
            small = [lat_norm, kept["query"][1], kept["d_query"][1]]
            got = wires.near_c(later(jnp.concatenate(small, 1), zero))
            lat, query, d_query = got[:, :width], got[:, width : width + quarter], got[:, width + quarter :]
            lift = wires.near_c(later(kept["d_lift"][group:], zero))
            lift = jnp.concatenate([kept["d_lift"][:group], lift], 0)
            query = jnp.concatenate([kept["query_x"][0], expand(query, local)], 0)
            g_key = (dot_rows(lift, query) * scale).astype(bf16)
            lat = jnp.concatenate([lat_norm, lat], 0)
            d_query = jnp.concatenate([kept["d_query"][0], d_query], 0)
            return [dot_rows(lat, d_query).astype(bf16), g_key]

        index = lax.broadcasted_iota(jnp.int32, (half, half), 0)
        goal = lax.broadcasted_iota(jnp.int32, (half, half), 1)
        head, within = index // size, index % size
        order = ((head % local) * 2 + head // local) * size + within
        shuffle = (order == goal).astype(bf16)

        def columns(v):
            n = v.shape[2]
            both = [jnp.concatenate([v[0, i], v[1, i]], 1) for i in range(2)]
            out = dot(jnp.concatenate(both, 0), shuffle)
            return jnp.concatenate([out[:n], out[n:]], 1)

        def finish(query, key, value, out):
            out = jnp.concatenate([out[:, 0], out[:, 1]], 2).reshape(shard, width).astype(f32)
            key_value = jnp.concatenate([columns(key), columns(value)], 1)
            return columns(query), key_value, out

        def finish_generic(query_key, g_value, g_output):
            blocks = jnp.concatenate(query_key + [g_value], 1).reshape(dp, shard, 3 * quarter)
            parts = lax.psum_scatter(blocks, "dp", scatter_dimension=0, tiled=False)
            whole = g_output.reshape(H // 2, 1, size, half)
            whole = wires.by_y(whole, jnp.zeros_like(whole), 1).reshape(dp, shard, half)
            out = lax.psum_scatter(whole, "dp", scatter_dimension=0, tiled=False)
            parts = lax.all_gather(parts, "section", axis=0).reshape(2, 2, shard, 3 * quarter)
            out = lax.all_gather(out, "section", axis=0).reshape(2, 2, shard, half)
            out = jnp.sum(out.astype(f32), 0)
            parts = [columns(parts[..., j * quarter : (j + 1) * quarter]) for j in range(3)]
            out = jnp.concatenate([out[0], out[1]], 1)
            return parts[0], jnp.concatenate(parts[1:], 1), out

        def ffn_grads(active, dz_all, mn_all, d_hidden):
            g_inner = dot_rows(mn_all, d_hidden).astype(bf16)
            return g_inner, dot_rows(active, dz_all).astype(bf16)

        def norm_latents(x_hat, level):
            return (x_hat * gains[level, 1] + biases[level, 1]).astype(bf16)

        def middle(x_rows, branch, level):
            branch = branch[:rows] + wires.near_y(branch[rows:].astype(bf16)).astype(f32)
            mid = (x_rows + branch).astype(bf16).astype(f32)
            hat_m, rstd_m = normed(mid)
            mn = (hat_m * gains[level, 2] + biases[level, 2]).astype(bf16)
            return mid, hat_m, rstd_m, mn

        def ffn_back(dz_all, hidden, level):
            d_active = dot_cols(dz_all, w_outer[level])
            return jax.vjp(gelu, hidden)[1](d_active)[0].astype(bf16)

        def middle_back(grad, hat_m, rstd_m, d_mn, level):
            d_low = (grad + norm_back(hat_m, rstd_m, d_mn * gains[level, 2])).astype(bf16)
            return d_low, jnp.concatenate([d_low, wires.near_y(d_low)], 0)

        def latents_back(d_low, d_lat, x_hat, x_rstd, level):
            d_norm = d_lat[:rows] + wires.near_y(d_lat[rows:].astype(bf16)).astype(f32)
            grad = d_low.astype(f32) + norm_back(x_hat, x_rstd, d_norm * gains[level, 1])
            if level > 0:
                grad = grad.astype(bf16).astype(f32)
            return d_norm, grad

        def vector_rows(attn, d_norm, x_hat, d_mn, hat_m):
            return [
                attn["d_gain"],
                jnp.sum(d_norm * x_hat, 0),
                jnp.sum(d_mn * hat_m, 0),
                attn["d_bias"],
                jnp.sum(d_norm, 0),
                jnp.sum(d_mn, 0),
            ]

        def media_pair(attn):
            left = jnp.concatenate([attn["ds"], attn["low"]], 0)
            return left, jnp.concatenate([attn["key_g"], attn["val_g"]], 0)

        def outputs(x_low, grad, media_grad, outs, sums):
            sums = sums.reshape(layers, 2, 3, shard)
            both = wires.spread(jnp.stack([x_low.astype(f32), grad]))
            return (
                both[:, 0].astype(bf16),
                media_grad,
                both[:, 1],
                *outs,
                sums[:, 0, :2],
                sums[:, 1, :2],
                sums[:, :, 2],
            )

        x_hat0, x_rstd0 = normed(state)
        lat_norm0 = norm_latents(x_hat0, 0)
        x_hat0, x_rstd0 = x_hat0[:rows], x_rstd0[:rows]
        x_rows0 = state[:rows]

        if not wires.hops:
            nil = Zero(jnp.zeros((1, 1), f32), 0)
            x_rows, x_hat, x_rstd, lat_norm = x_rows0, x_hat0, x_rstd0, lat_norm0
            kept = []
            for level in range(layers):
                got = [
                    lax.all_gather(picked[level, j], "dp", axis=0).reshape(width, quarter)
                    for j in range(3)
                ]
                out = lax.all_gather(w_output[level], "dp", axis=0, tiled=True)
                out = at(out.reshape(H // 2, 2, size, 2, half), y, 1)
                got.append(at(out, c, 2).reshape(half, half))
                weights = [[item, wires.near_c(item)] for item in got]
                w_in = wires.trade_all(inner_block(level, 1, 0, 0)).reshape(width, span)
                if level > 0:
                    x_hat, x_rstd = normed(x_rows)
                    mine = norm_latents(x_hat, level)
                    lat_norm = jnp.concatenate([mine, wires.near_y(mine)], 0)
                attn = look(lat_norm, weights[0], weights[1], level)
                branch = answer(attn, weights[2], weights[3])
                mid, hat_m, rstd_m, mn = middle(x_rows, branch, level)
                mn_all = wires.gather_rows(mn)
                hidden = dot(mn_all, w_in)
                active = gelu(hidden).astype(bf16)
                x_low = (mid + wires.sum_rows(dot(active, w_outer[level]))).astype(bf16)
                x_rows = x_low.astype(f32)
                kept.append(
                    (attn, lat_norm, x_hat, x_rstd, hat_m, rstd_m, mn_all, hidden, active, weights, w_in)
                )
            grad = target.astype(f32)
            ffn_out, attn_out, vector_grads, media_sum = [], [], [], 0.0
            for level in reversed(range(layers)):
                attn, lat_norm, x_hat, x_rstd, hat_m, rstd_m, mn_all, hidden, active, weights, w_in = kept[level]
                dz_all = wires.gather_rows(grad.astype(bf16))
                d_hidden = ffn_back(dz_all, hidden, level)
                d_mn = wires.sum_rows(dot_cols(d_hidden, w_in))
                share = ffn_grads(active, dz_all, mn_all, d_hidden)
                share = [lax.psum(v.astype(f32), "section") for v in share]
                inner = share[0].reshape(dp, shard, span).astype(bf16)
                inner = wires.trade_all(lambda d: inner[d])
                inner = jnp.transpose(inner, (1, 0, 2)).reshape(shard, dp * span)
                ffn_out.insert(0, (inner.astype(f32), share[1]))
                d_low, d_mid = middle_back(grad, hat_m, rstd_m, d_mn, level)
                answer_back(d_mid, lat_norm, weights, level, attn)
                d_lat = look_back(lat_norm, weights, level, attn)
                d_norm, grad = latents_back(d_low, d_lat, x_hat, x_rstd, level)
                vector_grads = vector_rows(attn, d_norm, x_hat, d_mn, hat_m) + vector_grads
                attn_out.insert(
                    0, finish_generic(query_grads(lat_norm, attn, nil), *value_grads(attn, nil))
                )
                media_sum = media_sum + dot_rows(*media_pair(attn))
            d_media = norm_back(hat.astype(f32), rstd_media, media_sum)
            got = wires.near_y(cut(d_media, half * (1 - y), half).astype(bf16))
            media_grad = wires.spread_c(cut(d_media, half * y, half) + got.astype(f32))
            extra = lax.psum(jnp.stack(vector_grads), "section")
            sums = lax.psum_scatter(extra, "dp", scatter_dimension=1, tiled=True)
            outs = [jnp.stack([attn_out[level][i] for level in range(layers)]) for i in range(3)]
            outs += [jnp.stack([ffn_out[level][i] for level in range(layers)]) for i in range(2)]
            return outputs(x_low, grad, media_grad, outs, sums)

        order = wires.trade_order()
        w_q, w_k = [weights_of(v) for v in first[:2]]
        attn0 = look(lat_norm0, w_q, w_k, 0)
        zero, (second,) = gate([attn0["low"]], [second])
        inner0 = wires.trade_far(inner0, zero)
        w_v, w_o = [weights_of(v) for v in (second[0], joined(second[1]))]
        weights0 = [w_q, w_k, w_v, w_o]
        branch = answer(attn0, w_v, w_o)
        zero, (branch,) = gate([inner0[1]], [branch])
        step = zero.index
        mid0, hat_m0, rstd_m0, mn = middle(x_rows0, branch, 0)
        mn_all0 = wires.gather_rows(mn)
        inner0 = place(inner0[0] + list(inner0[1]), [v + step for v in order], dp)
        inner0 = wires.by_c(inner0[:, None], wires.near_c(inner0)[:, None], 1)
        w_in0 = inner0.reshape(width, span)
        hidden0 = dot(mn_all0, w_in0)
        active0 = gelu(hidden0).astype(bf16)
        x_low = (mid0 + wires.sum_rows(dot(active0, w_outer[0]))).astype(bf16)

        zero, (x_low, rest) = gate([], [x_low, rest])
        inner1 = wires.trade_near(inner_block(1, 4, s, zero.index))
        targets = wires.gather_near(later(target, zero))
        x_rows1 = x_low.astype(f32)
        x_hat1, x_rstd1 = normed(x_rows1)
        mine = norm_latents(x_hat1, 1)
        lat_norm1 = jnp.concatenate([mine, wires.near_y(mine)], 0)
        weights1 = [weights_of(v) for v in (rest[0], rest[1], rest[2], joined(rest[3]))]
        attn1 = look(lat_norm1, weights1[0], weights1[1], 1)
        zero, _ = gate([attn1["low"]])
        inner1 = wires.trade_far(inner1, zero)
        targets = later(jnp.concatenate(targets, 0), zero)
        target_all = jnp.concatenate([targets, wires.send(targets, wires.swap_x)], 0)
        branch = answer(attn1, weights1[2], weights1[3])
        zero, (branch,) = gate([], [branch])
        step = zero.index
        mid1, hat_m1, rstd_m1, mn = middle(x_rows1, branch, 1)
        mn_all1 = wires.gather_rows(mn)
        inner1 = place(inner1[0] + list(inner1[1]), [v + step for v in order], dp)
        inner1 = wires.by_y(inner1[:, None], wires.near_y(inner1)[:, None], 1)
        inner1 = wires.by_c(inner1[:, :, None], wires.near_c(inner1)[:, :, None], 2)
        w_in1 = inner1.reshape(width, span)
        hidden1 = dot(mn_all1, w_in1)
        active1 = gelu(hidden1).astype(bf16)
        x_part = dot(active1, w_outer[1]).astype(bf16)

        d_hidden = ffn_back(target_all, hidden1, 1)
        d_mn1 = wires.sum_rows(dot_cols(d_hidden, w_in1))
        g_ffn = ffn_grads(active1, target_all, mn_all1, d_hidden)
        zero, (d_mn1,) = gate(g_ffn, [d_mn1])

        def shared(grads):
            g_inner = jnp.transpose(grads[0].reshape(dp, 4, part, span), (1, 0, 2, 3))
            parts = [g_inner, grads[1].reshape(4, span // 4, width)]
            return [lax.psum_scatter(v, "section", scatter_dimension=0) for v in parts]

        def output_blocks(grad):
            grad = grad.reshape(dp, size, half)
            return jnp.concatenate([grad[:, :, :quarter], grad[:, :, quarter:]], 1)

        def output_columns(v):
            v = v.reshape(2, 2, 2, size, quarter)
            return jnp.concatenate([v[:, :, 0], v[:, :, 1]], 3)

        share1 = shared(g_ffn)
        d_low1, d_mid1 = middle_back(target.astype(f32), hat_m1, rstd_m1, d_mn1, 1)
        answer_back(d_mid1, lat_norm1, weights1, 1, attn1)
        d_lat = look_back(lat_norm1, weights1, 1, attn1)
        zero, (d_lat,) = gate([], [d_lat])
        d_norm1, grad = latents_back(d_low1, d_lat, x_hat1, x_rstd1, 1)
        dz_all = wires.gather_rows(grad.astype(bf16))
        g_attn = query_grads(lat_norm1, attn1, zero) + value_grads(attn1, zero)

        zero, (dz_all,) = gate(g_attn, [dz_all])
        blocks = [v.reshape(dp, shard, quarter) for v in g_attn[:3]] + [output_blocks(g_attn[3])]
        blocks = jnp.concatenate(blocks, 2)
        blocks1 = lax.psum_scatter(blocks, "dp", scatter_dimension=0, tiled=False)
        d_hidden = ffn_back(dz_all, hidden0, 0)
        d_mn0 = wires.sum_rows(dot_cols(d_hidden, w_in0))
        g_ffn = ffn_grads(active0, dz_all, mn_all0, d_hidden)
        left, right = media_pair(attn1)
        media_sum = dot_rows(left, later(right, zero))
        zero, (d_mn0, *g_ffn) = gate([media_sum, *share1], [d_mn0, *g_ffn])
        share0 = shared(g_ffn)
        d_low0, d_mid0 = middle_back(grad, hat_m0, rstd_m0, d_mn0, 0)
        answer_back(d_mid0, lat_norm0, weights0, 0, attn0)
        g_vo = value_grads(attn0, zero)
        zero, (attn0["shift"],) = gate(g_vo, [attn0["shift"]])
        g_vo = jnp.concatenate([g_vo[0].reshape(dp, shard, quarter), output_blocks(g_vo[1])], 2)
        g_vo = wires.sum_far(g_vo, zero.index)
        d_lat = look_back(lat_norm0, weights0, 0, attn0)
        zero, (d_lat, attn0["d_lift"]) = gate([], [d_lat, attn0["d_lift"]])
        d_norm0, grad = latents_back(d_low0, d_lat, x_hat0, x_rstd0, 0)
        left, right = media_pair(attn0)
        media_sum = media_sum + dot_rows(left, later(right, zero))
        d_media = norm_back(hat.astype(f32), rstd_media, media_sum)
        send = cut(d_media, half * (1 - y), half).astype(bf16)
        zero, (send, grad, attn0["d_lift"]) = gate([g_vo[1]], [send, grad, attn0["d_lift"]])
        got = wires.near_y(send)
        g_vo = wires.sum_near(g_vo[0], later(g_vo[1], zero))
        x_part = wires.sum_rows(later(x_part, zero).astype(f32))
        extra = vector_rows(attn0, d_norm0, x_hat0, d_mn0, hat_m0)
        extra += vector_rows(attn1, d_norm1, x_hat1, d_mn1, hat_m1)
        extra = jnp.zeros((128, width), f32).at[: layers * 6].set(jnp.stack(extra)).T
        g_qk = query_grads(lat_norm0, attn0, zero) + [extra.astype(bf16)]
        g_qk = jnp.concatenate(g_qk, 1)
        zero, (g_qk, blocks1, *share1) = gate([], [g_qk, blocks1, *share1])
        step = zero.index
        g_qk = wires.sum_far(g_qk.reshape(dp, shard, g_qk.shape[1]), step)
        blocks1 = lax.all_gather(blocks1, "section", axis=0)
        outer1 = lax.all_gather(share1[1], "section", axis=0, tiled=True)
        zero, (far, grad, share0[0]) = gate([*g_vo[1], x_part], [g_qk[1], grad, share0[0]])
        step = zero.index
        g_qk = wires.sum_near(g_qk[0], far)
        blocks1 = later(blocks1, zero).reshape(2, 2, shard, 4 * quarter)
        parts = [blocks1[..., j * quarter : (j + 1) * quarter] for j in range(4)]
        attn_out1 = finish(*parts[:3], output_columns(parts[3]))
        zero, (outer0,) = gate(attn_out1, [share0[1]])
        outer0 = lax.all_gather(outer0, "section", axis=0, tiled=True)
        step = zero.index
        trade = jnp.concatenate([share1[0], share0[0]], 1)
        trade = wires.trade_near(lambda d: at(trade, d + step))
        outs = [jnp.zeros((layers,) + v.shape, f32).at[1].set(v) for v in attn_out1]
        zero, (grad, *arrived) = gate([], [grad, *g_qk[1], *outs])
        arrived, outs = arrived[:-3], arrived[-3:]
        g_qk = (g_qk[0], arrived)
        trade = wires.trade_far(trade, zero)
        x_out = (mid1 + x_part + zero.value).astype(bf16)

        def summed(mine, parts):
            for v in parts:
                mine = mine + v.astype(f32)
            return mine.astype(bf16)

        four = jnp.concatenate([summed(*g_vo), summed(*g_qk)], 1)
        four_y = wires.near_y(four)
        inner = []
        for i in range(layers):
            rows_of = slice(i * part, (i + 1) * part)
            inner.append(line_up([v[rows_of] for v in trade[0] + list(trade[1])], order))
        inner = jnp.stack(inner)
        zero, _ = gate([inner])
        inner = lax.all_gather(inner, "section", axis=0)
        four = wires.by_y(four[None], later(four_y, zero)[None], 0)
        four = wires.by_c(four[:, None], wires.near_c(four)[:, None], 1)
        value, out, query, key = [four[..., i * quarter : (i + 1) * quarter] for i in range(4)]
        sums = jnp.sum(four[..., 4 * quarter :].astype(f32), axis=(0, 1))[:, : layers * 6].T
        inner = [inner[:, i].reshape(shard, dp * span).astype(f32) for i in range(layers)]
        ffn_out = [(inner[1], outer0.astype(f32)), (inner[0], outer1.astype(f32))]
        attn_out0 = finish(query, key, value, output_columns(out))
        media_grad = wires.spread_c(cut(d_media, half * y, half) + later(got, zero).astype(f32))
        outs = [v.at[0].set(u) for v, u in zip(outs, attn_out0)]
        outs += [jnp.stack([ffn_out[level][i] for level in range(layers)]) for i in range(2)]
        return outputs(x_out, grad, media_grad, outs, sums)

    return run


def solution(mesh):
    wires = Wires(mesh.shape["dp"], mesh.shape["section"])
    return jax.shard_map(
        shards(wires),
        mesh=mesh,
        in_specs=(
            P("dp", None, "section"),
            P("dp", None, None),
            P("dp"),
            P("dp", None, "section"),
            P(None, "dp", None),
            P(None, "dp", None),
            P(None, "dp", None),
            P(None, "dp", None),
            P(None, "dp", None),
            P(None, None, "dp"),
            P(None, None, "dp"),
        ),
        out_specs=(
            P("dp", None, "section"),
            P("dp", None, "section"),
            P("dp", None, "section"),
            P(None, "dp", None),
            P(None, "dp", None),
            P(None, "dp", None),
            P(None, "dp", None),
            P(None, "dp", None),
            P(None, None, "dp"),
            P(None, None, "dp"),
            P(None, None, "dp"),
        ),
        check_vma=False,
    )
```
